128 devices in a mesh: row: 8 (over z, core), col: 16 (over y, x).
Axes of the slice: x: 4, y: 4, z: 4, core: 2. Of those that a mesh axis runs over, the one named last changes fastest.
Arguments:
- frame_blocks: float32 [8, 256, 3, 128, 128], P('row', 'col'), may hold values from 0 to 1
- block_routes: int32 [8, 256], P('row', 'col'), may hold values from 0 to 31, as said below
- seam_labels: int32 [1024, 2048], P('row', 'col'), may hold values from 0 to 31, as said below
Outputs:
- panorama: float32 [3, 1024, 2048], P(None, 'row', 'col')
The draws below stay inside these ranges and needn't reach their ends.
Inputs may be any that keep to these rules, and one draw needn't show every extreme that they name: `block_routes`: on each device the 16 blocks name distinct slots; slot s below 16 means tile column s of the same tile row, 16 + s means tile column s of the next tile row; devices of the last tile row use only slots below 16; every device uses the slot equal to its own column index. `seam_labels`: every label names a slot of its tile into which a block was sent.
All inputs are finite; a program needn't handle non-finite values.
Results may differ from the reference program's by a relative error of at most 0.0003.
Values sent between devices are 32-bit elements; how exact they have to be, the bound alone decides.
No kernel may reach another device: no remote copies, remote signals or barrier semaphores. Data moves between devices by JAX's collectives and lax.ppermute only.
A program may use at most 192 MiB of HBM per device.

```python
import jax
import jax.numpy as jnp
from jax import lax

CHANNELS = 3
TP = 128
LEVELS = 6
FB = 16
N_ROW = 8
N_COL = 16


def chosen_slots(key):
    slot_total = 2 * N_COL
    base_key = jax.random.fold_in(key, 11)
    slot_ids = jnp.arange(slot_total, dtype=jnp.int32)[None, None, :]
    col_ids = jnp.arange(N_COL, dtype=jnp.int32)[None, :, None]
    row_ids = jnp.arange(N_ROW, dtype=jnp.int32)[:, None, None]
    scores = jax.random.randint(base_key, (N_ROW, N_COL, slot_total), 0, 2 ** 20) * 64 + slot_ids
    scores = jnp.where(slot_ids == col_ids, -1, scores)
    scores = scores + jnp.where((row_ids == N_ROW - 1) & (slot_ids >= N_COL), 2 ** 30, 0)
    ordered = jnp.argsort(scores, axis=-1, stable=True)[:, :, :FB]
    return ordered.astype(jnp.int32)


def draw_block_routes(key, part):
    chosen = chosen_slots(key)
    return chosen.reshape(N_ROW, N_COL * FB)


def draw_seam_labels(key, part):
    chosen = chosen_slots(key)
    key = jax.random.fold_in(key, 2)
    slot_total = 2 * N_COL
    hits = jnp.any(chosen[:, :, :, None] == jnp.arange(slot_total, dtype=jnp.int32)[None, None, None, :], axis=2)
    same_row = jnp.transpose(hits[:, :, :N_COL], (0, 2, 1))
    above = jnp.transpose(hits[:, :, N_COL:], (0, 2, 1))
    from_above = jnp.concatenate([jnp.zeros((1, N_COL, N_COL), dtype=bool), above[:-1]], axis=0)
    live = jnp.concatenate([same_row, from_above], axis=2)
    tallied_hits = jnp.sum(live.astype(jnp.int32), axis=-1)
    table = jnp.argsort(jnp.where(live, 0, 1) * 64 + jnp.arange(slot_total, dtype=jnp.int32)[None, None, :], axis=-1, stable=True).astype(jnp.int32)
    picks = jax.random.randint(key, (N_ROW, N_COL, TP, TP), 0, tallied_hits[:, :, None, None])
    tile_ids = jnp.arange(N_ROW, dtype=jnp.int32)[:, None] * N_COL + jnp.arange(N_COL, dtype=jnp.int32)[None, :]
    flat_index = tile_ids[:, :, None, None] * slot_total + picks
    labels = table.reshape(-1)[flat_index]
    return jnp.transpose(labels, (0, 2, 1, 3)).reshape(N_ROW * TP, N_COL * TP).astype(jnp.int32)


def block_scale(rng, extent, split, smallest, high):
    gain, own = 1.0, jax.random.fold_in(rng, 6)
    for position, parts in split:
        steps = jnp.exp(jax.random.uniform(jax.random.fold_in(own, position), (parts,), jnp.float32, smallest / len(split), high / len(split)))
        gain = gain * jnp.repeat(steps, extent[position] // parts).reshape([-1 if axis == position else 1 for axis in range(len(extent))])
    return gain


def setup_inputs(seed: int = 0) -> dict:
    key_list = jax.random.split(jax.random.key(seed), 4)
    frame_blocks = jnp.clip(1.0 * jax.random.uniform(key_list[0], (N_ROW, N_COL * FB, CHANNELS, TP, TP), jnp.float32) ** block_scale(key_list[0], (N_ROW, N_COL * FB, CHANNELS, TP, TP), ((0, 8), (1, 16)), -0.2, 0.2), 0.0, 1.0)
    block_routes = draw_block_routes(jax.random.fold_in(key_list[3], 71), 0)
    seam_labels = draw_seam_labels(jax.random.fold_in(key_list[3], 71), 0)
    return dict(frame_blocks=frame_blocks, block_routes=block_routes, seam_labels=seam_labels)


def halve_grid(sample_entries):
    height, width = sample_entries.shape[-2:]
    shaped = sample_entries.reshape(sample_entries.shape[:-2] + (height // 2, 2, width // 2, 2))
    return shaped.mean(axis=(-3, -1))


def upsample(sample_entries):
    return jnp.repeat(jnp.repeat(sample_entries, 2, axis=-2), 2, axis=-1)


def band_sums(blocks, labels, start_slot):
    slot_ids = start_slot + jnp.arange(blocks.shape[0], dtype=jnp.int32)
    mask_factors = (labels[None, :, :] == slot_ids[:, None, None]).astype(jnp.float32)
    soften_filter = blocks
    totals = []
    for octave in range(LEVELS):
        if octave < LEVELS - 1:
            broad_scale_layer = halve_grid(soften_filter)
            detail = soften_filter - upsample(broad_scale_layer)
        else:
            detail = soften_filter
        totals.append(jnp.sum(detail * mask_factors[:, None, :, :], axis=0))
        if octave < LEVELS - 1:
            soften_filter = broad_scale_layer
            mask_factors = halve_grid(mask_factors)
    return totals


def collapse(totals):
    picture = totals[-1]
    for detail_band in reversed(totals[:-1]):
        picture = upsample(picture) + detail_band
    return picture


def reference(frame_blocks, block_routes, seam_labels):
    stacked = frame_blocks.reshape(N_ROW, N_COL, FB, CHANNELS, TP, TP)
    routes = block_routes.reshape(N_ROW, N_COL, FB)
    sources = jnp.arange(N_COL)
    rows_out = []
    for row_index in range(N_ROW):
        def tile_picture(column):
            pieces = []
            for offset in range(2):
                source_row = row_index - offset
                if source_row < 0:
                    pieces.append(jnp.zeros((N_COL, CHANNELS, TP, TP), jnp.float32))
                else:
                    matches = routes[source_row] == offset * N_COL + column
                    picked = jnp.argmax(matches, axis=1).astype(jnp.int32)
                    present = jnp.any(matches, axis=1)
                    selected = stacked[source_row][sources, picked]
                    pieces.append(jnp.where(present[:, None, None, None], selected, jnp.float32(0.0)))
            labels_tile = lax.dynamic_slice(seam_labels, (jnp.asarray(row_index * TP, jnp.int32), (column * TP).astype(jnp.int32)), (TP, TP))
            return collapse(band_sums(jnp.concatenate(pieces, axis=0), labels_tile, 0))
        panel_canvases = lax.map(tile_picture, jnp.arange(N_COL, dtype=jnp.int32))
        rows_out.append(jnp.transpose(panel_canvases, (1, 2, 0, 3)).reshape(CHANNELS, TP, N_COL * TP))
    return jnp.concatenate(rows_out, axis=1)
```

```python
import functools

import jax
import jax.numpy as jnp
import ml_dtypes
import numpy as np
from jax import lax
from jax.experimental import pallas as pl
from jax.experimental.pallas import tpu as pltpu
from jax.sharding import PartitionSpec as P

LEVELS = 6
SIDE = 4
TILE = 128
HALF = TILE // 2
CH = 3
ROWS = CH * TILE
PAIRED = CH * HALF
BOTH = ("row", "col")
AXES = dict(rows=8, cols=16)

STARTS = {1: 0, 2: 64, 3: 96, 4: 112, 5: 120, 6: 124}


def pooling_matrices():
    x = np.arange(TILE)
    pool = np.zeros((TILE, 3 * TILE), np.float32)
    spread = np.zeros((TILE, TILE), np.float32)
    for k in range(1, LEVELS):
        for i in range(TILE >> k):
            lane = STARTS[k] + i
            pool[(x >> k) == i, lane] = 0.25**k
            spread[lane, (x >> k) == i] = 1.0
            if k < LEVELS - 1:
                pool[(x >> (k + 1)) == (i >> 1), TILE + lane] = 0.25 ** (k + 1)
    for i in range(TILE):
        pool[(x >> 1) == (i >> 1), 2 * TILE + i] = 0.25
    twice = lambda m: np.concatenate([m, m], axis=0).astype(ml_dtypes.bfloat16)
    return twice(pool), twice(spread)


def split_two(value):
    high = value.astype(jnp.bfloat16)
    low = (value - high.astype(jnp.float32)).astype(jnp.bfloat16)
    return jnp.concatenate([high, low], axis=1)


def even(ref, count):
    return ref[pl.ds(0, count, stride=2), :]


def odd(ref, count):
    return ref[pl.ds(1, count, stride=2), :]


def slot_contribution(x_ref, label_ref, slot_ids, pool_ref, spread_ref, scratch):
    n = len(slot_ids)
    a_refs, b_refs, m_refs, w_refs, up_ref = scratch
    x_even, x_odd = even(x_ref, n * PAIRED), odd(x_ref, n * PAIRED)
    label_even, label_odd = even(label_ref, n * HALF), odd(label_ref, n * HALF)
    hit_even, hit_odd = [], []
    for j, slot in enumerate(slot_ids):
        hit_even.append(label_even[j * HALF : (j + 1) * HALF] == slot)
        hit_odd.append(label_odd[j * HALF : (j + 1) * HALF] == slot)
    one, zero = jnp.float32(1), jnp.float32(0)
    mask = jnp.concatenate(
        [jnp.where(e, one, zero) + jnp.where(o, one, zero) for e, o in zip(hit_even, hit_odd)], axis=0
    )
    pooled = jnp.dot(split_two(x_even + x_odd), pool_ref[...], preferred_element_type=jnp.float32)
    a = {1: pooled[:, :TILE]}
    b = {1: pooled[:, TILE : 2 * TILE]}
    first = pooled[:, 2 * TILE :]
    m = {
        1: jnp.dot(
            mask.astype(jnp.bfloat16), pool_ref[:TILE, :TILE], preferred_element_type=jnp.float32
        )
    }
    for k in range(1, LEVELS - 1):
        for values, refs, rows in ((a, a_refs, n * PAIRED), (b, b_refs, n * PAIRED), (m, m_refs, n * HALF)):
            count = rows >> (k - 1)
            refs[k][...] = values[k]
            values[k + 1] = even(refs[k], count // 2) + odd(refs[k], count // 2)
    weights = {}
    for k in range(1, LEVELS):
        count = HALF >> (k - 1)
        for j in range(n):
            for c in range(CH):
                w_refs[k][pl.ds((j * CH + c) * count, count), :] = m[k][j * count : (j + 1) * count]
        weights[k] = w_refs[k][...]
    picture = None
    for k in range(LEVELS - 1, 0, -1):
        rows = (n * PAIRED) >> (k - 1)
        lane = lax.broadcasted_iota(jnp.int32, (rows, TILE), 1)
        inside = (lane >= STARTS[k]) & (lane < STARTS[k + 1])
        if k == LEVELS - 1:
            spread_up = jnp.zeros((rows, TILE), jnp.float32)
        else:
            lower = (lane[: rows // 2] >= STARTS[k]) & (lane[: rows // 2] < STARTS[k + 1])
            merged = jnp.where(lower, b[k + 1], picture)
            up_ref[pl.ds(0, rows // 2, stride=2), :] = merged
            up_ref[pl.ds(1, rows // 2, stride=2), :] = merged
            spread_up = up_ref[pl.ds(0, rows), :]
        weight = weights[k]
        banded = jnp.where(weight > 0, (a[k] - spread_up) * weight, zero)
        picture = jnp.where(inside, banded, spread_up)
    wide = jnp.dot(split_two(picture), spread_ref[...], preferred_element_type=jnp.float32)
    x_even, x_odd = x_even - first, x_odd - first
    out_even, out_odd = [], []
    for j in range(n):
        for c in range(CH):
            rows = slice((j * CH + c) * HALF, (j * CH + c + 1) * HALF)
            out_even.append(jnp.where(hit_even[j], x_even[rows], zero) + wide[rows])
            out_odd.append(jnp.where(hit_odd[j], x_odd[rows], zero) + wide[rows])
    return out_even, out_odd


def blend_kernel(batch, messages, has_sum, groups, source_ref, *refs):
    message_refs = refs[:messages]
    label_ref, pool_ref, spread_ref = refs[messages : messages + 3]
    refs = refs[messages + 3 :]
    sum_ref = None
    if has_sum:
        sum_ref, refs = refs[0], refs[1:]
    out_refs, refs = refs[:groups], refs[groups:]
    levels = LEVELS - 1
    a_refs = dict(zip(range(1, levels), refs[: levels - 1]))
    b_refs = dict(zip(range(1, levels), refs[levels - 1 : 2 * levels - 2]))
    m_refs = dict(zip(range(1, levels), refs[2 * levels - 2 : 3 * levels - 3]))
    w_refs = dict(zip(range(1, levels + 1), refs[3 * levels - 3 : 4 * levels - 3]))
    up_ref = refs[4 * levels - 3]
    scratch = (a_refs, b_refs, m_refs, w_refs, up_ref)
    step = pl.program_id(0)
    even_sum = odd_sum = None
    for i, message_ref in enumerate(message_refs):
        slot_ids = [source_ref[i] + (j % 2) * SIDE * SIDE for j in range(batch)]
        even_part, odd_part = slot_contribution(message_ref, label_ref, slot_ids, pool_ref, spread_ref, scratch)
        even_sum = even_part if i == 0 else [p + q for p, q in zip(even_sum, even_part)]
        odd_sum = odd_part if i == 0 else [p + q for p, q in zip(odd_sum, odd_part)]
    for g, out_ref in enumerate(out_refs):

        def store():
            for j in range(batch):
                for c in range(CH):
                    rows = pl.ds(c * HALF, HALF)
                    for parity, part in ((0, even_sum), (1, odd_sum)):
                        value = part[j * CH + c]
                        if has_sum:
                            value = value + sum_ref[j, parity, rows, :]
                        out_ref[j, parity, rows, :] = value

        if groups == 1:
            store()
        else:
            pl.when(step == g)(store)


def blend(messages, sources, labels, pool, spread, total, groups):
    batch = 2
    steps = 2 * SIDE // batch
    part = (batch, 2, PAIRED, TILE)
    here = lambda i, s: (i, 0)
    fixed = lambda i, s: (0, 0)
    in_specs = [pl.BlockSpec((batch * ROWS, TILE), here) for _ in messages]
    in_specs += [
        pl.BlockSpec((batch * TILE, TILE), here),
        pl.BlockSpec(pool.shape, fixed),
        pl.BlockSpec(spread.shape, fixed),
    ]
    operands = list(messages) + [labels, pool, spread]
    if total is not None:
        in_specs.append(pl.BlockSpec(part, lambda i, s: (i, 0, 0, 0)))
        operands.append(total)
    if groups == 1:
        out_specs = [pl.BlockSpec(part, lambda i, s: (i, 0, 0, 0))]
        out_shape = [jax.ShapeDtypeStruct((2 * SIDE, 2, PAIRED, TILE), jnp.float32)]
    else:
        out_specs = [pl.BlockSpec(part, lambda i, s: (0, 0, 0, 0)) for _ in range(groups)]
        out_shape = [jax.ShapeDtypeStruct(part, jnp.float32) for _ in range(groups)]
    image = lambda rows: pltpu.VMEM((rows, TILE), jnp.float32)
    scratch = [image((batch * PAIRED) >> (k - 1)) for _ in range(2) for k in range(1, LEVELS - 1)]
    scratch += [image((batch * HALF) >> (k - 1)) for k in range(1, LEVELS - 1)]
    scratch += [image((batch * PAIRED) >> (k - 1)) for k in range(1, LEVELS)]
    scratch += [image(batch * PAIRED)]
    slots = 2 * SIDE * len(messages)
    out = pl.pallas_call(
        functools.partial(blend_kernel, batch, len(messages), total is not None, groups),
        grid_spec=pltpu.PrefetchScalarGridSpec(
            num_scalar_prefetch=1,
            grid=(steps,),
            in_specs=in_specs,
            out_specs=out_specs,
            scratch_shapes=scratch,
        ),
        out_shape=out_shape,
        compiler_params=pltpu.CompilerParams(vmem_limit_bytes=48 * 2**20),
        cost_estimate=pl.CostEstimate(
            flops=slots * PAIRED * 2 * 256 * 512, bytes_accessed=slots * ROWS * TILE * 12, transcendentals=0
        ),
    )(sources, *operands)
    return out[0] if groups == 1 else out


def route_kernel(route_ref, block_ref, *refs):
    out_refs, sems = refs[:SIDE], refs[SIDE]
    count = block_ref.shape[0]
    for i in range(count):
        target, slot = route_ref[0, i], route_ref[1, i]
        for d in range(SIDE):

            @pl.when(target == d)
            def _():
                pltpu.make_async_copy(block_ref.at[i], out_refs[d].at[slot], sems.at[i]).start()

    for i in range(count):
        pltpu.make_async_copy(block_ref.at[i], out_refs[0].at[0], sems.at[i]).wait()


def route(blocks, targets):
    out_shape = [jax.ShapeDtypeStruct((2 * SIDE, ROWS, TILE), jnp.float32) for _ in range(SIDE)]
    return pl.pallas_call(
        route_kernel,
        in_specs=[pl.BlockSpec(memory_space=pltpu.SMEM), pl.BlockSpec(memory_space=pl.ANY)],
        out_specs=[pl.BlockSpec(memory_space=pl.ANY) for _ in range(SIDE)],
        out_shape=out_shape,
        scratch_shapes=[pltpu.SemaphoreType.DMA((blocks.shape[0],))],
    )(targets, blocks)


def finish_kernel(own_ref, first_ref, second_ref, third_ref, above_ref, out_ref):
    for parity in range(2):
        total = own_ref[0, parity] + first_ref[0, parity] + second_ref[0, parity] + third_ref[0, parity]
        out_ref[pl.ds(parity, PAIRED, stride=2), :] = total + above_ref[parity]


def finish(own, first, second, third, above):
    part = pl.BlockSpec((1, 2, PAIRED, TILE), lambda i: (0, 0, 0, 0))
    return pl.pallas_call(
        finish_kernel,
        grid=(1,),
        in_specs=[part] * 4 + [pl.BlockSpec((2, PAIRED, TILE), lambda i: (0, 0, 0))],
        out_specs=pl.BlockSpec((ROWS, TILE), lambda i: (0, 0)),
        out_shape=jax.ShapeDtypeStruct((ROWS, TILE), jnp.float32),
    )(own, first, second, third, above)


def pairs(phase, steps):
    result = []
    for r in range(AXES["rows"]):
        for c in range(AXES["cols"]):
            y, x = divmod(c, SIDE)
            if r % 2 == phase:
                x = (x + steps) % SIDE
            else:
                y = (y + steps) % SIDE
            result.append((r * AXES["cols"] + c, r * AXES["cols"] + y * SIDE + x))
    return result


def moved(value, phase, steps):
    return lax.ppermute(value, BOTH, pairs(phase, steps))


def shards(frame_blocks, block_routes, seam_labels):
    rows, columns = AXES["rows"], AXES["cols"]
    pool, spread = (jnp.asarray(m) for m in pooling_matrices())
    along_x = lax.axis_index("row") % 2 == 0
    column = lax.axis_index("col")
    y, x = column // SIDE, column % SIDE
    near = jnp.where(along_x, x, y)
    far = jnp.where(along_x, y, x)

    wanted = block_routes[0]
    wanted_y, wanted_x = (wanted % columns) // SIDE, wanted % SIDE
    wanted_near = jnp.where(along_x, wanted_x, wanted_y)
    wanted_far = jnp.where(along_x, wanted_y, wanted_x)
    slot = ((wanted_far - far) % SIDE) * 2 + wanted // columns
    targets = jnp.stack([(wanted_near - near) % SIDE, slot])
    messages = route(frame_blocks[0].reshape(-1, ROWS, TILE), targets)

    next_labels = lax.ppermute(seam_labels, "row", [(r + 1, r) for r in range(rows - 1)])
    two_labels = jnp.stack([seam_labels, next_labels])
    labels = jnp.concatenate([two_labels] + [moved(two_labels, 1, -d) for d in range(1, SIDE)])
    labels = labels.reshape(-1, TILE)

    arrived = [messages[0]] + [moved(messages[d], 0, d) for d in range(1, SIDE)]
    arrived = [m.reshape(-1, TILE) for m in arrived]
    sources = []
    for d in range(SIDE):
        from_near = (near - d) % SIDE
        sources.append(jnp.where(along_x, far * SIDE + from_near, from_near * SIDE + far))
    source = lambda *ds: jnp.stack([sources[d] for d in ds]).astype(jnp.int32)
    total = blend([arrived[0]], source(0), labels, pool, spread, None, 1)
    total = blend([arrived[1], arrived[3]], source(1, 3), labels, pool, spread, total, 1)
    parts = blend([arrived[2]], source(2), labels, pool, spread, total, SIDE)
    got = [parts[0]] + [moved(parts[d], 1, d) for d in range(1, SIDE)]
    spilled = got[0][1] + got[1][1] + got[2][1] + got[3][1]
    above = lax.ppermute(spilled, "row", [(r, r + 1) for r in range(rows - 1)])
    return finish(*got, above).reshape(CH, TILE, TILE)


def solution(mesh):
    return jax.shard_map(
        shards,
        mesh=mesh,
        in_specs=(P("row", "col", None, None, None), P("row", "col"), P("row", "col")),
        out_specs=P(None, "row", "col"),
        check_vma=False,
    )
```

```python
import functools

import jax
import jax.numpy as jnp
import ml_dtypes
import numpy as np
from jax import lax
from jax.experimental import pallas as pl
from jax.experimental.pallas import tpu as pltpu
from jax.sharding import PartitionSpec as P

LEVELS = 6
SIDE = 4
TILE = 128
HALF = TILE // 2
CH = 3
ROWS = CH * TILE
PAIRED = CH * HALF
BOTH = ("row", "col")
AXES = dict(rows=8, cols=16)
BATCH = 2
LIMIT = 16 * 2**20

STARTS = {1: 0, 2: 64, 3: 96, 4: 112, 5: 120, 6: 124}


def pooling_matrices():
    x = np.arange(TILE)
    pool = np.zeros((TILE, 3 * TILE), np.float32)
    spread = np.zeros((TILE, TILE), np.float32)
    for k in range(1, LEVELS):
        for i in range(TILE >> k):
            lane = STARTS[k] + i
            pool[(x >> k) == i, lane] = 0.25**k
            spread[lane, (x >> k) == i] = 1.0
            if k < LEVELS - 1:
                pool[(x >> (k + 1)) == (i >> 1), TILE + lane] = 0.25 ** (k + 1)
    for i in range(TILE):
        pool[(x >> 1) == (i >> 1), 2 * TILE + i] = 0.25
    twice = lambda m: np.concatenate([m, m], axis=0).astype(ml_dtypes.bfloat16)
    return twice(pool), twice(spread)


def split_two(value):
    high = value.astype(jnp.bfloat16)
    low = (value - high.astype(jnp.float32)).astype(jnp.bfloat16)
    return jnp.concatenate([high, low], axis=1)


def even(ref, count):
    return ref[pl.ds(0, count, stride=2), :]


def odd(ref, count):
    return ref[pl.ds(1, count, stride=2), :]


def slot_contribution(x_ref, label_ref, slot_ids, pool_ref, spread_ref, scratch):
    n = len(slot_ids)
    a_refs, b_refs, m_refs, w_refs, up_ref = scratch
    x_even, x_odd = even(x_ref, n * PAIRED), odd(x_ref, n * PAIRED)
    label_even, label_odd = even(label_ref, n * HALF), odd(label_ref, n * HALF)
    hit_even, hit_odd = [], []
    for j, slot in enumerate(slot_ids):
        hit_even.append(label_even[j * HALF : (j + 1) * HALF] == slot)
        hit_odd.append(label_odd[j * HALF : (j + 1) * HALF] == slot)
    one, zero = jnp.float32(1), jnp.float32(0)
    mask = jnp.concatenate(
        [jnp.where(e, one, zero) + jnp.where(o, one, zero) for e, o in zip(hit_even, hit_odd)], axis=0
    )
    pooled = jnp.dot(split_two(x_even + x_odd), pool_ref[...], preferred_element_type=jnp.float32)
    a = {1: pooled[:, :TILE]}
    b = {1: pooled[:, TILE : 2 * TILE]}
    first = pooled[:, 2 * TILE :]
    m = {
        1: jnp.dot(
            mask.astype(jnp.bfloat16), pool_ref[:TILE, :TILE], preferred_element_type=jnp.float32
        )
    }
    for k in range(1, LEVELS - 1):
        for values, refs, rows in ((a, a_refs, n * PAIRED), (b, b_refs, n * PAIRED), (m, m_refs, n * HALF)):
            count = rows >> (k - 1)
            refs[k][...] = values[k]
            values[k + 1] = even(refs[k], count // 2) + odd(refs[k], count // 2)
    weights = {}
    for k in range(1, LEVELS):
        count = HALF >> (k - 1)
        for j in range(n):
            for c in range(CH):
                w_refs[k][pl.ds((j * CH + c) * count, count), :] = m[k][j * count : (j + 1) * count]
        weights[k] = w_refs[k][...]
    picture = None
    for k in range(LEVELS - 1, 0, -1):
        rows = (n * PAIRED) >> (k - 1)
        lane = lax.broadcasted_iota(jnp.int32, (rows, TILE), 1)
        inside = (lane >= STARTS[k]) & (lane < STARTS[k + 1])
        if k == LEVELS - 1:
            spread_up = jnp.zeros((rows, TILE), jnp.float32)
        else:
            lower = (lane[: rows // 2] >= STARTS[k]) & (lane[: rows // 2] < STARTS[k + 1])
            merged = jnp.where(lower, b[k + 1], picture)
            up_ref[pl.ds(0, rows // 2, stride=2), :] = merged
            up_ref[pl.ds(1, rows // 2, stride=2), :] = merged
            spread_up = up_ref[pl.ds(0, rows), :]
        weight = weights[k]
        banded = jnp.where(weight > 0, (a[k] - spread_up) * weight, zero)
        picture = jnp.where(inside, banded, spread_up)
    wide = jnp.dot(split_two(picture), spread_ref[...], preferred_element_type=jnp.float32)
    x_even, x_odd = x_even - first, x_odd - first
    out_even, out_odd = [], []
    for j in range(n):
        for c in range(CH):
            rows = slice((j * CH + c) * HALF, (j * CH + c + 1) * HALF)
            out_even.append(jnp.where(hit_even[j], x_even[rows], zero) + wide[rows])
            out_odd.append(jnp.where(hit_odd[j], x_odd[rows], zero) + wide[rows])
    return out_even, out_odd


def place():
    column = lax.axis_index("col")
    y, x = column // SIDE, column % SIDE
    along_x = lax.axis_index("row") % 2 == 0
    return jnp.where(along_x, x, y), jnp.where(along_x, y, x), along_x


def blend_kernel(offsets, has_sum, groups, next_row, *refs):
    count = len(offsets)
    message_refs = refs[:count]
    label_ref, pool_ref, spread_ref = refs[count : count + 3]
    refs = refs[count + 3 :]
    sum_ref = None
    if has_sum:
        sum_ref, refs = refs[0], refs[1:]
    out_refs, refs = refs[:groups], refs[groups:]
    levels = LEVELS - 1
    a_refs = dict(zip(range(1, levels), refs[: levels - 1]))
    b_refs = dict(zip(range(1, levels), refs[levels - 1 : 2 * levels - 2]))
    m_refs = dict(zip(range(1, levels), refs[2 * levels - 2 : 3 * levels - 3]))
    w_refs = dict(zip(range(1, levels + 1), refs[3 * levels - 3 : 4 * levels - 3]))
    up_ref = refs[4 * levels - 3]
    scratch = (a_refs, b_refs, m_refs, w_refs, up_ref)
    near, far, along_x = place()
    slots = []
    for offset in offsets:
        from_near = (near - offset + SIDE) % SIDE
        source = jnp.where(along_x, far * SIDE + from_near, from_near * SIDE + far)
        slots.append(source + next_row * SIDE * SIDE)

    def step(i):
        even_sum = odd_sum = None
        labels = label_ref.at[pl.ds(i * BATCH * TILE, BATCH * TILE)]
        for message_ref, slot in zip(message_refs, slots):
            message = message_ref.at[pl.ds(i * BATCH * ROWS, BATCH * ROWS)]
            even_part, odd_part = slot_contribution(message, labels, [slot] * BATCH, pool_ref, spread_ref, scratch)
            even_sum = even_part if even_sum is None else [p + q for p, q in zip(even_sum, even_part)]
            odd_sum = odd_part if odd_sum is None else [p + q for p, q in zip(odd_sum, odd_part)]
        for j in range(BATCH):
            for c in range(CH):
                rows = pl.ds(c * HALF, HALF)
                for parity, part in ((0, even_sum), (1, odd_sum)):
                    value = part[j * CH + c]
                    if has_sum:
                        value = value + sum_ref[i * BATCH + j, parity, rows, :]
                    if groups == 1:
                        out_refs[0][i * BATCH + j, parity, rows, :] = value
                    else:
                        out_refs[i * BATCH + j][parity, rows, :] = value

    if groups == 1:
        pl.loop(0, SIDE // BATCH)(step)
    else:
        for i in range(SIDE // BATCH):
            step(i)


def blend(messages, offsets, labels, matrices, total, groups, next_row):
    part = (2, PAIRED, TILE)
    operands = list(messages) + [labels] + list(matrices) + ([] if total is None else [total])
    if groups == 1:
        out_shape = [jax.ShapeDtypeStruct((SIDE, *part), jnp.float32)]
    else:
        out_shape = [jax.ShapeDtypeStruct(part, jnp.float32) for _ in range(groups)]
    image = lambda rows: pltpu.VMEM((rows, TILE), jnp.float32)
    scratch = [image((BATCH * PAIRED) >> (k - 1)) for _ in range(2) for k in range(1, LEVELS - 1)]
    scratch += [image((BATCH * HALF) >> (k - 1)) for k in range(1, LEVELS - 1)]
    scratch += [image((BATCH * PAIRED) >> (k - 1)) for k in range(1, LEVELS)]
    scratch += [image(BATCH * PAIRED)]
    slots = SIDE * len(messages)
    whole = pl.BlockSpec(memory_space=pltpu.VMEM)
    out = pl.pallas_call(
        functools.partial(blend_kernel, offsets, total is not None, groups, next_row),
        in_specs=[whole] * len(operands),
        out_specs=[whole] * groups,
        scratch_shapes=scratch,
        out_shape=out_shape,
        compiler_params=pltpu.CompilerParams(vmem_limit_bytes=LIMIT),
        cost_estimate=pl.CostEstimate(
            flops=slots * PAIRED * 2 * 256 * 512, bytes_accessed=slots * ROWS * TILE * 12, transcendentals=0
        ),
    )(*operands)
    return out[0] if groups == 1 else out


def route_kernel(route_ref, block_ref, *refs):
    out_refs, (found_ref, sem) = refs[: 2 * SIDE], refs[2 * SIDE :]
    columns = SIDE * SIDE
    near, far, along_x = place()
    for q in range(2 * columns):
        found_ref[q] = -1
    for i in range(block_ref.shape[0]):
        found_ref[route_ref[0, i]] = i
    for next_row in (1, 0):
        for d in range(SIDE):
            there = (near + d) % SIDE
            for slot in range(SIDE):
                across = (far + slot) % SIDE
                column = jnp.where(along_x, across * SIDE + there, there * SIDE + across)
                block = found_ref[next_row * columns + column]

                @pl.when(block >= 0)
                def _():
                    target = out_refs[next_row * SIDE + d].at[slot]
                    pltpu.make_async_copy(block_ref.at[block], target, sem).start()

    pltpu.make_async_copy(block_ref, block_ref, sem).wait()


def route(blocks, routes):
    out_shape = [jax.ShapeDtypeStruct((SIDE, ROWS, TILE), jnp.float32) for _ in range(2 * SIDE)]
    out = pl.pallas_call(
        route_kernel,
        in_specs=[pl.BlockSpec(memory_space=pltpu.SMEM), pl.BlockSpec(memory_space=pltpu.HBM)],
        out_specs=[pl.BlockSpec(memory_space=pltpu.VMEM) for _ in out_shape],
        out_shape=out_shape,
        scratch_shapes=[pltpu.SMEM((2 * SIDE * SIDE,), jnp.int32), pltpu.SemaphoreType.DMA],
        compiler_params=pltpu.CompilerParams(vmem_limit_bytes=LIMIT),
        cost_estimate=pl.CostEstimate(flops=0, bytes_accessed=2 * blocks.size * 4, transcendentals=0),
    )(routes, blocks)
    return out[:SIDE], out[SIDE:]


def finish_kernel(own_ref, first_ref, second_ref, third_ref, above_ref, out_ref):
    for parity in range(2):
        total = own_ref[parity] + first_ref[parity] + second_ref[parity] + third_ref[parity]
        out_ref[pl.ds(parity, PAIRED, stride=2), :] = total + above_ref[parity]


def finish(*parts):
    whole = pl.BlockSpec(memory_space=pltpu.VMEM)
    return pl.pallas_call(
        finish_kernel,
        in_specs=[whole] * len(parts),
        out_specs=whole,
        out_shape=jax.ShapeDtypeStruct((ROWS, TILE), jnp.float32),
        compiler_params=pltpu.CompilerParams(vmem_limit_bytes=LIMIT),
    )(*parts)


def pairs(phase, steps):
    result = []
    for r in range(AXES["rows"]):
        for c in range(AXES["cols"]):
            y, x = divmod(c, SIDE)
            if r % 2 == phase:
                x = (x + steps) % SIDE
            else:
                y = (y + steps) % SIDE
            result.append((r * AXES["cols"] + c, r * AXES["cols"] + y * SIDE + x))
    return result


def moved(value, phase, steps):
    return lax.ppermute(value, BOTH, pairs(phase, steps))


def shards(frame_blocks, block_routes, seam_labels):
    rows = AXES["rows"]
    matrices = [jnp.asarray(m) for m in pooling_matrices()]
    blocks = frame_blocks[0].reshape(-1, ROWS, TILE)
    next_labels = lax.ppermute(seam_labels, "row", [(r + 1, r) for r in range(rows - 1)])
    two_labels = jnp.stack([seam_labels, next_labels])
    labels = [two_labels] + [moved(two_labels, 1, -d) for d in range(1, SIDE)]
    tiles = [jnp.concatenate([pair[i] for pair in labels]) for i in range(2)]

    got = [None, None]
    routed = route(blocks, block_routes)
    for next_row in (1, 0):
        messages = routed[next_row]
        arrived = [messages[0]] + [moved(messages[d], 0, d) for d in range(1, SIDE)]
        arrived = [m.reshape(-1, TILE) for m in arrived]
        label = tiles[next_row]
        total = blend([arrived[0]], (0,), label, matrices, None, 1, next_row)
        total = blend([arrived[1], arrived[3]], (1, 3), label, matrices, total, 1, next_row)
        parts = blend([arrived[2]], (2,), label, matrices, total, SIDE, next_row)
        got[next_row] = [parts[0]] + [moved(parts[d], 1, d) for d in range(1, SIDE)]
    spilled = sum(got[1][1:], got[1][0])
    above = lax.ppermute(spilled, "row", [(r, r + 1) for r in range(rows - 1)])
    return finish(*got[0], above).reshape(CH, TILE, TILE)


def solution(mesh):
    return jax.shard_map(
        shards,
        mesh=mesh,
        in_specs=(P("row", "col", None, None, None), P("row", "col"), P("row", "col")),
        out_specs=P(None, "row", "col"),
        check_vma=False,
    )
```

```python
import functools

import jax
import jax.numpy as jnp
import ml_dtypes
import numpy as np
from jax import lax
from jax.experimental import pallas as pl
from jax.experimental.pallas import tpu as pltpu
from jax.sharding import PartitionSpec as P

LEVELS = 6
SIDE = 4
TILE = 128
HALF = TILE // 2
CH = 3
ROWS = CH * TILE
PAIRED = CH * HALF
BOTH = ("row", "col")
AXES = dict(rows=8, cols=16)
BATCH = 2
NEXT_FIRST = (1, 0)
LIMIT = 16 * 2**20
ROUTE_LIMIT = 56 * 2**20

STARTS = {1: 0, 2: 64, 3: 96, 4: 112, 5: 120, 6: 124}


def pooling_matrices():
    x = np.arange(TILE)
    pool = np.zeros((TILE, 3 * TILE), np.float32)
    spread = np.zeros((TILE, TILE), np.float32)
    for k in range(1, LEVELS):
        for i in range(TILE >> k):
            lane = STARTS[k] + i
            pool[(x >> k) == i, lane] = 0.25**k
            spread[lane, (x >> k) == i] = 1.0
            if k < LEVELS - 1:
                pool[(x >> (k + 1)) == (i >> 1), TILE + lane] = 0.25 ** (k + 1)
    for i in range(TILE):
        pool[(x >> 1) == (i >> 1), 2 * TILE + i] = 0.25
    twice = lambda m: np.concatenate([m, m], axis=0).astype(ml_dtypes.bfloat16)
    return twice(pool), twice(spread)


def split_two(value):
    high = value.astype(jnp.bfloat16)
    low = (value - high.astype(jnp.float32)).astype(jnp.bfloat16)
    return jnp.concatenate([high, low], axis=1)


def even(ref, count):
    return ref[pl.ds(0, count, stride=2), :]


def odd(ref, count):
    return ref[pl.ds(1, count, stride=2), :]


def slot_contribution(x_ref, label_ref, slot_ids, pool_ref, spread_ref, scratch):
    n = len(slot_ids)
    a_refs, b_refs, m_refs, w_refs, up_ref = scratch
    x_even, x_odd = even(x_ref, n * PAIRED), odd(x_ref, n * PAIRED)
    label_even, label_odd = even(label_ref, n * HALF), odd(label_ref, n * HALF)
    hit_even, hit_odd = [], []
    for j, slot in enumerate(slot_ids):
        hit_even.append(label_even[j * HALF : (j + 1) * HALF] == slot)
        hit_odd.append(label_odd[j * HALF : (j + 1) * HALF] == slot)
    one, zero = jnp.float32(1), jnp.float32(0)
    mask = jnp.concatenate(
        [jnp.where(e, one, zero) + jnp.where(o, one, zero) for e, o in zip(hit_even, hit_odd)], axis=0
    )
    pooled = jnp.dot(split_two(x_even + x_odd), pool_ref[...], preferred_element_type=jnp.float32)
    a = {1: pooled[:, :TILE]}
    b = {1: pooled[:, TILE : 2 * TILE]}
    first = pooled[:, 2 * TILE :]
    m = {
        1: jnp.dot(
            mask.astype(jnp.bfloat16), pool_ref[:TILE, :TILE], preferred_element_type=jnp.float32
        )
    }
    for k in range(1, LEVELS - 1):
        for values, refs, rows in ((a, a_refs, n * PAIRED), (b, b_refs, n * PAIRED), (m, m_refs, n * HALF)):
            count = rows >> (k - 1)
            refs[k][...] = values[k]
            values[k + 1] = even(refs[k], count // 2) + odd(refs[k], count // 2)
    weights = {}
    for k in range(1, LEVELS):
        count = HALF >> (k - 1)
        for j in range(n):
            for c in range(CH):
                w_refs[k][pl.ds((j * CH + c) * count, count), :] = m[k][j * count : (j + 1) * count]
        weights[k] = w_refs[k][...]
    picture = None
    for k in range(LEVELS - 1, 0, -1):
        rows = (n * PAIRED) >> (k - 1)
        lane = lax.broadcasted_iota(jnp.int32, (rows, TILE), 1)
        inside = (lane >= STARTS[k]) & (lane < STARTS[k + 1])
        if k == LEVELS - 1:
            spread_up = jnp.zeros((rows, TILE), jnp.float32)
        else:
            lower = (lane[: rows // 2] >= STARTS[k]) & (lane[: rows // 2] < STARTS[k + 1])
            merged = jnp.where(lower, b[k + 1], picture)
            up_ref[pl.ds(0, rows // 2, stride=2), :] = merged
            up_ref[pl.ds(1, rows // 2, stride=2), :] = merged
            spread_up = up_ref[pl.ds(0, rows), :]
        weight = weights[k]
        banded = jnp.where(weight > 0, (a[k] - spread_up) * weight, zero)
        picture = jnp.where(inside, banded, spread_up)
    wide = jnp.dot(split_two(picture), spread_ref[...], preferred_element_type=jnp.float32)
    x_even, x_odd = x_even - first, x_odd - first
    out_even, out_odd = [], []
    for j in range(n):
        for c in range(CH):
            rows = slice((j * CH + c) * HALF, (j * CH + c + 1) * HALF)
            out_even.append(jnp.where(hit_even[j], x_even[rows], zero) + wide[rows])
            out_odd.append(jnp.where(hit_odd[j], x_odd[rows], zero) + wide[rows])
    return out_even, out_odd


def place():
    column = lax.axis_index("col")
    y, x = column // SIDE, column % SIDE
    along_x = lax.axis_index("row") % 2 == 0
    return jnp.where(along_x, x, y), jnp.where(along_x, y, x), along_x


def blend_kernel(offsets, has_sum, row, *refs):
    groups = 1 if row is None else SIDE
    count = len(offsets)
    message_refs = refs[:count]
    label_ref, pool_ref, spread_ref = refs[count : count + 3]
    refs = refs[count + 3 :]
    sum_ref = None
    if has_sum:
        sum_ref, refs = refs[0], refs[1:]
    out_refs, refs = refs[:groups], refs[groups:]
    levels = LEVELS - 1
    a_refs = dict(zip(range(1, levels), refs[: levels - 1]))
    b_refs = dict(zip(range(1, levels), refs[levels - 1 : 2 * levels - 2]))
    m_refs = dict(zip(range(1, levels), refs[2 * levels - 2 : 3 * levels - 3]))
    w_refs = dict(zip(range(1, levels + 1), refs[3 * levels - 3 : 4 * levels - 3]))
    up_ref = refs[4 * levels - 3]
    scratch = (a_refs, b_refs, m_refs, w_refs, up_ref)
    near, far, along_x = place()
    slots = []
    for offset in offsets:
        from_near = (near - offset + SIDE) % SIDE
        source = jnp.where(along_x, far * SIDE + from_near, from_near * SIDE + far)
        slots.append(source)

    def step(i, next_row):
        even_sum = odd_sum = None
        labels = label_ref.at[pl.ds(i * BATCH * TILE, BATCH * TILE)]
        for message_ref, slot in zip(message_refs, slots):
            message = message_ref.at[pl.ds(i * BATCH * ROWS, BATCH * ROWS)]
            even_part, odd_part = slot_contribution(message, labels, [slot + next_row * SIDE * SIDE] * BATCH, pool_ref, spread_ref, scratch)
            even_sum = even_part if even_sum is None else [p + q for p, q in zip(even_sum, even_part)]
            odd_sum = odd_part if odd_sum is None else [p + q for p, q in zip(odd_sum, odd_part)]
        for j in range(BATCH):
            for c in range(CH):
                rows = pl.ds(c * HALF, HALF)
                for parity, part in ((0, even_sum), (1, odd_sum)):
                    value = part[j * CH + c]
                    if has_sum:
                        value = value + sum_ref[i * BATCH + j, parity, rows, :]
                    if groups == 1:
                        out_refs[0][i * BATCH + j, parity, rows, :] = value
                    else:
                        out_refs[i * BATCH + j - row * SIDE][parity, rows, :] = value

    for part in range(2):
        start, stop = part * SIDE // BATCH, (part + 1) * SIDE // BATCH
        if row is None:
            pl.loop(start, stop)(functools.partial(step, next_row=NEXT_FIRST[part]))
        elif row == part:
            for i in range(start, stop):
                step(i, NEXT_FIRST[part])


def blend(messages, offsets, labels, matrices, total, row):
    groups = 1 if row is None else SIDE
    part = (2, PAIRED, TILE)
    operands = list(messages) + [labels] + list(matrices) + ([] if total is None else [total])
    if groups == 1:
        out_shape = [jax.ShapeDtypeStruct((2 * SIDE, *part), jnp.float32)]
    else:
        out_shape = [jax.ShapeDtypeStruct(part, jnp.float32) for _ in range(groups)]
    image = lambda rows: pltpu.VMEM((rows, TILE), jnp.float32)
    scratch = [image((BATCH * PAIRED) >> (k - 1)) for _ in range(2) for k in range(1, LEVELS - 1)]
    scratch += [image((BATCH * HALF) >> (k - 1)) for k in range(1, LEVELS - 1)]
    scratch += [image((BATCH * PAIRED) >> (k - 1)) for k in range(1, LEVELS)]
    scratch += [image(BATCH * PAIRED)]
    slots = (2 if row is None else 1) * SIDE * len(messages)
    whole = pl.BlockSpec(memory_space=pltpu.VMEM)
    out = pl.pallas_call(
        functools.partial(blend_kernel, offsets, total is not None, row),
        in_specs=[whole] * len(operands),
        out_specs=[whole] * groups,
        scratch_shapes=scratch,
        out_shape=out_shape,
        compiler_params=pltpu.CompilerParams(vmem_limit_bytes=LIMIT),
        cost_estimate=pl.CostEstimate(
            flops=slots * PAIRED * 2 * 256 * 512, bytes_accessed=slots * ROWS * TILE * 12, transcendentals=0
        ),
    )(*operands)
    return out[0] if groups == 1 else out


def route_kernel(offsets, labelled, route_ref, block_ref, *refs):
    if labelled:
        label_refs, refs = refs[:2], refs[2:]
        two_ref, refs = refs[len(offsets)], refs[: len(offsets)] + refs[len(offsets) + 1 :]
    out_refs, (found_ref, sem) = refs[: len(offsets)], refs[len(offsets) :]
    columns = SIDE * SIDE
    near, far, along_x = place()
    for q in range(2 * columns):
        found_ref[q] = -1
    for i in range(block_ref.shape[0]):
        found_ref[route_ref[0, i]] = i
    count = 0
    for out_ref, d in zip(out_refs, offsets):
        there = (near + d) % SIDE
        for slot in range(SIDE):
            across = (far + slot) % SIDE
            column = jnp.where(along_x, across * SIDE + there, there * SIDE + across)
            for row in range(2):
                block = found_ref[NEXT_FIRST[row] * columns + column]
                count += jnp.where(block >= 0, 1, 0)

                @pl.when(block >= 0)
                def _():
                    pltpu.make_async_copy(block_ref.at[block], out_ref.at[row * SIDE + slot], sem).start()

    if labelled:
        for i in range(2):
            two_ref[i] = label_refs[i][...]

    @pl.loop(0, count)
    def _(_):
        pltpu.make_async_copy(block_ref.at[0], out_refs[0].at[0], sem).wait()


def route(blocks, routes, offsets, labels):
    out_shape = [jax.ShapeDtypeStruct((2 * SIDE, ROWS, TILE), jnp.float32) for _ in offsets]
    whole = pl.BlockSpec(memory_space=pltpu.VMEM)
    if labels:
        out_shape.append(jax.ShapeDtypeStruct((2, TILE, TILE), jnp.int32))
    return pl.pallas_call(
        functools.partial(route_kernel, offsets, len(labels) > 0),
        in_specs=[pl.BlockSpec(memory_space=pltpu.SMEM), pl.BlockSpec(memory_space=pltpu.HBM)]
        + [whole] * len(labels),
        out_specs=[whole] * len(out_shape),
        out_shape=out_shape,
        scratch_shapes=[pltpu.SMEM((2 * SIDE * SIDE,), jnp.int32), pltpu.SemaphoreType.DMA],
        compiler_params=pltpu.CompilerParams(vmem_limit_bytes=ROUTE_LIMIT),
        cost_estimate=pl.CostEstimate(flops=0, bytes_accessed=blocks.size * 4, transcendentals=0),
    )(routes, blocks, *labels)


def finish_kernel(own_ref, first_ref, second_ref, third_ref, above_ref, out_ref):
    for parity in range(2):
        total = own_ref[parity] + first_ref[parity] + second_ref[parity] + third_ref[parity]
        out_ref[pl.ds(parity, PAIRED, stride=2), :] = total + above_ref[parity]


def finish(*parts):
    whole = pl.BlockSpec(memory_space=pltpu.VMEM)
    return pl.pallas_call(
        finish_kernel,
        in_specs=[whole] * len(parts),
        out_specs=whole,
        out_shape=jax.ShapeDtypeStruct((ROWS, TILE), jnp.float32),
        compiler_params=pltpu.CompilerParams(vmem_limit_bytes=LIMIT),
    )(*parts)


def pairs(phase, steps):
    result = []
    for r in range(AXES["rows"]):
        for c in range(AXES["cols"]):
            y, x = divmod(c, SIDE)
            if r % 2 == phase:
                x = (x + steps) % SIDE
            else:
                y = (y + steps) % SIDE
            result.append((r * AXES["cols"] + c, r * AXES["cols"] + y * SIDE + x))
    return result


def moved(value, phase, steps):
    return lax.ppermute(value, BOTH, pairs(phase, steps))


def shards(frame_blocks, block_routes, seam_labels):
    rows = AXES["rows"]
    matrices = [jnp.asarray(m) for m in pooling_matrices()]
    blocks = frame_blocks[0].reshape(-1, ROWS, TILE)
    next_labels = lax.ppermute(seam_labels, "row", [(r + 1, r) for r in range(rows - 1)])
    here, opposite = route(blocks, block_routes, (0, 2), [])
    opposite = moved(opposite, 0, 2)
    up, back, two_labels = route(blocks, block_routes, (1, 3), [next_labels, seam_labels])
    labels = [two_labels] + [moved(two_labels, 1, -d) for d in range(1, SIDE)]
    up, back = moved(up, 0, 1), moved(back, 0, 3)
    here, up, back, opposite = (m.reshape(-1, TILE) for m in (here, up, back, opposite))
    tiles = jnp.concatenate([pair[row] for row in range(2) for pair in labels])
    total = blend([here, opposite], (0, 2), tiles, matrices, None, None)
    gathered = []
    for row in range(2):
        parts = blend([up, back], (1, 3), tiles, matrices, total, row)
        gathered.append([parts[0]] + [moved(parts[d], 1, d) for d in range(1, SIDE)])
    spilled = sum(gathered[0][1:], gathered[0][0])
    above = lax.ppermute(spilled, "row", [(r, r + 1) for r in range(rows - 1)])
    return finish(*gathered[1], above).reshape(CH, TILE, TILE)


def solution(mesh):
    return jax.shard_map(
        shards,
        mesh=mesh,
        in_specs=(P("row", "col", None, None, None), P("row", "col"), P("row", "col")),
        out_specs=P(None, "row", "col"),
        check_vma=False,
    )
```

```python
import functools

import jax
import jax.numpy as jnp
import ml_dtypes
import numpy as np
from jax import lax
from jax.experimental import pallas as pl
from jax.experimental.pallas import tpu as pltpu
from jax.sharding import PartitionSpec as P

LEVELS = 6
SIDE = 4
TILE = 128
HALF = TILE // 2
CH = 3
ROWS = CH * TILE
PAIRED = CH * HALF
BOTH = ("row", "col")
AXES = dict(rows=8, cols=16)
BATCH = 2
LIMIT = 16 * 2**20
ROUTE_LIMIT = 56 * 2**20

STARTS = {1: 0, 2: 64, 3: 96, 4: 112, 5: 120, 6: 124}


def pooling_matrices():
    x = np.arange(TILE)
    pool = np.zeros((TILE, 3 * TILE), np.float32)
    spread = np.zeros((TILE, TILE), np.float32)
    for k in range(1, LEVELS):
        for i in range(TILE >> k):
            lane = STARTS[k] + i
            pool[(x >> k) == i, lane] = 0.25**k
            spread[lane, (x >> k) == i] = 1.0
            if k < LEVELS - 1:
                pool[(x >> (k + 1)) == (i >> 1), TILE + lane] = 0.25 ** (k + 1)
    for i in range(TILE):
        pool[(x >> 1) == (i >> 1), 2 * TILE + i] = 0.25
    twice = lambda m: np.concatenate([m, m], axis=0).astype(ml_dtypes.bfloat16)
    return twice(pool), twice(spread)


def split_two(value):
    high = value.astype(jnp.bfloat16)
    low = (value - high.astype(jnp.float32)).astype(jnp.bfloat16)
    return jnp.concatenate([high, low], axis=1)


def even(ref, count):
    return ref[pl.ds(0, count, stride=2), :]


def odd(ref, count):
    return ref[pl.ds(1, count, stride=2), :]


def slot_contribution(x_ref, label_ref, slot_ids, pool_ref, spread_ref, scratch):
    n = len(slot_ids)
    a_refs, b_refs, m_refs, w_refs, up_ref = scratch
    x_even, x_odd = even(x_ref, n * PAIRED), odd(x_ref, n * PAIRED)
    label_even, label_odd = even(label_ref, n * HALF), odd(label_ref, n * HALF)
    hit_even, hit_odd = [], []
    for j, slot in enumerate(slot_ids):
        hit_even.append(label_even[j * HALF : (j + 1) * HALF] == slot)
        hit_odd.append(label_odd[j * HALF : (j + 1) * HALF] == slot)
    one, zero = jnp.float32(1), jnp.float32(0)
    mask = jnp.concatenate(
        [jnp.where(e, one, zero) + jnp.where(o, one, zero) for e, o in zip(hit_even, hit_odd)], axis=0
    )
    pooled = jnp.dot(split_two(x_even + x_odd), pool_ref[...], preferred_element_type=jnp.float32)
    a = {1: pooled[:, :TILE]}
    b = {1: pooled[:, TILE : 2 * TILE]}
    first = pooled[:, 2 * TILE :]
    m = {
        1: jnp.dot(
            mask.astype(jnp.bfloat16), pool_ref[:TILE, :TILE], preferred_element_type=jnp.float32
        )
    }
    for k in range(1, LEVELS - 1):
        for values, refs, rows in ((a, a_refs, n * PAIRED), (b, b_refs, n * PAIRED), (m, m_refs, n * HALF)):
            count = rows >> (k - 1)
            refs[k][...] = values[k]
            values[k + 1] = even(refs[k], count // 2) + odd(refs[k], count // 2)
    weights = {}
    for k in range(1, LEVELS):
        count = HALF >> (k - 1)
        for j in range(n):
            for c in range(CH):
                w_refs[k][pl.ds((j * CH + c) * count, count), :] = m[k][j * count : (j + 1) * count]
        weights[k] = w_refs[k][...]
    picture = None
    for k in range(LEVELS - 1, 0, -1):
        rows = (n * PAIRED) >> (k - 1)
        lane = lax.broadcasted_iota(jnp.int32, (rows, TILE), 1)
        inside = (lane >= STARTS[k]) & (lane < STARTS[k + 1])
        if k == LEVELS - 1:
            spread_up = jnp.zeros((rows, TILE), jnp.float32)
        else:
            lower = (lane[: rows // 2] >= STARTS[k]) & (lane[: rows // 2] < STARTS[k + 1])
            merged = jnp.where(lower, b[k + 1], picture)
            up_ref[pl.ds(0, rows // 2, stride=2), :] = merged
            up_ref[pl.ds(1, rows // 2, stride=2), :] = merged
            spread_up = up_ref[pl.ds(0, rows), :]
        weight = weights[k]
        banded = jnp.where(weight > 0, (a[k] - spread_up) * weight, zero)
        picture = jnp.where(inside, banded, spread_up)
    wide = jnp.dot(split_two(picture), spread_ref[...], preferred_element_type=jnp.float32)
    x_even, x_odd = x_even - first, x_odd - first
    out_even, out_odd = [], []
    for j in range(n):
        for c in range(CH):
            rows = slice((j * CH + c) * HALF, (j * CH + c + 1) * HALF)
            out_even.append(jnp.where(hit_even[j], x_even[rows], zero) + wide[rows])
            out_odd.append(jnp.where(hit_odd[j], x_odd[rows], zero) + wide[rows])
    return out_even, out_odd


def place(below):
    column = lax.axis_index("col")
    y, x = column // SIDE, column % SIDE
    along_x = lax.axis_index("row") % 2 == below
    return jnp.where(along_x, x, y), jnp.where(along_x, y, x), along_x


def blend_kernel(offsets, totals, groups, below, *refs):
    count = len(offsets)
    message_refs = refs[:count]
    label_ref, pool_ref, spread_ref = refs[count : count + 3]
    refs = refs[count + 3 :]
    sum_refs, refs = refs[:totals], refs[totals:]
    out_refs, refs = refs[:groups], refs[groups:]
    levels = LEVELS - 1
    a_refs = dict(zip(range(1, levels), refs[: levels - 1]))
    b_refs = dict(zip(range(1, levels), refs[levels - 1 : 2 * levels - 2]))
    m_refs = dict(zip(range(1, levels), refs[2 * levels - 2 : 3 * levels - 3]))
    w_refs = dict(zip(range(1, levels + 1), refs[3 * levels - 3 : 4 * levels - 3]))
    up_ref = refs[4 * levels - 3]
    scratch = (a_refs, b_refs, m_refs, w_refs, up_ref)
    near, far, along_x = place(below)
    slots = []
    for offset in offsets:
        from_near = (near - offset + SIDE) % SIDE
        source = jnp.where(along_x, far * SIDE + from_near, from_near * SIDE + far)
        slots.append(source + below * SIDE * SIDE)

    def step(i):
        even_sum = odd_sum = None
        labels = label_ref.at[pl.ds(i * BATCH * TILE, BATCH * TILE)]
        for message_ref, slot in zip(message_refs, slots):
            message = message_ref.at[pl.ds(i * BATCH * ROWS, BATCH * ROWS)]
            even_part, odd_part = slot_contribution(message, labels, [slot] * BATCH, pool_ref, spread_ref, scratch)
            even_sum = even_part if even_sum is None else [p + q for p, q in zip(even_sum, even_part)]
            odd_sum = odd_part if odd_sum is None else [p + q for p, q in zip(odd_sum, odd_part)]
        for j in range(BATCH):
            for c in range(CH):
                rows = pl.ds(c * HALF, HALF)
                for parity, part in ((0, even_sum), (1, odd_sum)):
                    value = part[j * CH + c]
                    for sum_ref in sum_refs:
                        value = value + sum_ref[i * BATCH + j, parity, rows, :]
                    if groups == 1:
                        out_refs[0][i * BATCH + j, parity, rows, :] = value
                    else:
                        out_refs[i * BATCH + j][parity, rows, :] = value

    if groups == 1:
        pl.loop(0, SIDE // BATCH)(step)
    else:
        for i in range(SIDE // BATCH):
            step(i)


def blend(messages, offsets, labels, matrices, totals, groups, below):
    part = (2, PAIRED, TILE)
    operands = list(messages) + [labels] + list(matrices) + list(totals)
    if groups == 1:
        out_shape = [jax.ShapeDtypeStruct((SIDE, *part), jnp.float32)]
    else:
        out_shape = [jax.ShapeDtypeStruct(part, jnp.float32) for _ in range(groups)]
    image = lambda rows: pltpu.VMEM((rows, TILE), jnp.float32)
    scratch = [image((BATCH * PAIRED) >> (k - 1)) for _ in range(2) for k in range(1, LEVELS - 1)]
    scratch += [image((BATCH * HALF) >> (k - 1)) for k in range(1, LEVELS - 1)]
    scratch += [image((BATCH * PAIRED) >> (k - 1)) for k in range(1, LEVELS)]
    scratch += [image(BATCH * PAIRED)]
    slots = SIDE * len(messages)
    whole = pl.BlockSpec(memory_space=pltpu.VMEM)
    out = pl.pallas_call(
        functools.partial(blend_kernel, offsets, len(totals), groups, below),
        in_specs=[whole] * len(operands),
        out_specs=[whole] * groups,
        scratch_shapes=scratch,
        out_shape=out_shape,
        compiler_params=pltpu.CompilerParams(vmem_limit_bytes=LIMIT),
        cost_estimate=pl.CostEstimate(
            flops=slots * PAIRED * 2 * 256 * 512, bytes_accessed=slots * ROWS * TILE * 12, transcendentals=0
        ),
    )(*operands)
    return out[0] if groups == 1 else out


def route_kernel(pieces, after, route_ref, block_ref, *refs):
    refs = refs[after:]
    out_refs, (found_ref, sem) = refs[: len(pieces)], refs[len(pieces) :]
    columns = SIDE * SIDE
    for q in range(2 * columns):
        found_ref[q] = -1
    for i in range(block_ref.shape[0]):
        found_ref[route_ref[0, i]] = i
    count = 0
    for out_ref, (d, below) in zip(out_refs, pieces):
        near, far, along_x = place(below)
        there = (near + d) % SIDE
        for slot in range(SIDE):
            across = (far + slot) % SIDE
            column = jnp.where(along_x, across * SIDE + there, there * SIDE + across)
            block = found_ref[below * columns + column]
            count += jnp.where(block >= 0, 1, 0)

            @pl.when(block >= 0)
            def _():
                pltpu.make_async_copy(block_ref.at[block], out_ref.at[slot], sem).start()

    @pl.loop(0, count)
    def _(_):
        pltpu.make_async_copy(block_ref.at[0], out_refs[0].at[0], sem).wait()


def route(blocks, routes, pieces, after=()):
    out_shape = [jax.ShapeDtypeStruct((SIDE, ROWS, TILE), jnp.float32) for _ in pieces]
    whole = pl.BlockSpec(memory_space=pltpu.VMEM)
    return pl.pallas_call(
        functools.partial(route_kernel, pieces, len(after)),
        in_specs=[pl.BlockSpec(memory_space=pltpu.SMEM), pl.BlockSpec(memory_space=pltpu.HBM)]
        + [whole] * len(after),
        out_specs=[whole] * len(out_shape),
        out_shape=out_shape,
        scratch_shapes=[pltpu.SMEM((2 * SIDE * SIDE,), jnp.int32), pltpu.SemaphoreType.DMA],
        compiler_params=pltpu.CompilerParams(vmem_limit_bytes=ROUTE_LIMIT),
        cost_estimate=pl.CostEstimate(flops=0, bytes_accessed=blocks.size * 4, transcendentals=0),
    )(routes, blocks, *after)


def finish_kernel(own_ref, first_ref, second_ref, third_ref, out_ref):
    for parity in range(2):
        total = own_ref[parity] + first_ref[parity] + second_ref[parity] + third_ref[parity]
        out_ref[pl.ds(parity, PAIRED, stride=2), :] = total


def finish(*parts):
    whole = pl.BlockSpec(memory_space=pltpu.VMEM)
    return pl.pallas_call(
        finish_kernel,
        in_specs=[whole] * len(parts),
        out_specs=whole,
        out_shape=jax.ShapeDtypeStruct((ROWS, TILE), jnp.float32),
        compiler_params=pltpu.CompilerParams(vmem_limit_bytes=LIMIT),
    )(*parts)


def pairs(phase, steps):
    result = []
    for r in range(AXES["rows"]):
        for c in range(AXES["cols"]):
            y, x = divmod(c, SIDE)
            if r % 2 == phase:
                x = (x + steps) % SIDE
            else:
                y = (y + steps) % SIDE
            result.append((r * AXES["cols"] + c, r * AXES["cols"] + y * SIDE + x))
    return result


def moved(value, phase, steps):
    return lax.ppermute(value, BOTH, pairs(phase, steps))


def shards(frame_blocks, block_routes, seam_labels):
    rows = AXES["rows"]
    matrices = [jnp.asarray(m) for m in pooling_matrices()]
    blocks = frame_blocks[0].reshape(-1, ROWS, TILE)
    labels = jnp.concatenate([seam_labels] + [moved(seam_labels, 1, -d) for d in range(1, SIDE)])
    labels_below = lax.ppermute(labels, "row", [(r + 1, r) for r in range(rows - 1)])
    near, routed = {}, []
    for pieces in ([(0, 1), (2, 1)], [(1, 1), (3, 1)], [(0, 0), (1, 0), (3, 0), (2, 0)]):
        after = [labels, *routed[:1]] if near else []
        routed = route(blocks, block_routes, pieces, after)
        for (d, below), value in zip(pieces, routed):
            near[d, below] = (moved(value, below, d) if d else value).reshape(-1, TILE)
    down, own = ([near[d, below] for d in (0, 2, 1, 3)] for below in (1, 0))
    total = blend(down[:2], (0, 2), labels_below, matrices, [], 1, 1)
    total = blend(down[2:], (1, 3), labels_below, matrices, [total], 1, 1)
    above = lax.ppermute(total, "row", [(r, r + 1) for r in range(rows - 1)])
    total = blend(own[:2], (0, 2), labels, matrices, [], 1, 0)
    parts = blend(own[2:], (1, 3), labels, matrices, [total, above], SIDE, 0)
    return finish(parts[0], *[moved(parts[d], 1, d) for d in range(1, SIDE)]).reshape(CH, TILE, TILE)


def solution(mesh):
    return jax.shard_map(
        shards,
        mesh=mesh,
        in_specs=(P("row", "col", None, None, None), P("row", "col"), P("row", "col")),
        out_specs=P(None, "row", "col"),
        check_vma=False,
    )
```

```python
import functools

import jax
import jax.numpy as jnp
import ml_dtypes
import numpy as np
from jax import lax
from jax.experimental import pallas as pl
from jax.experimental.pallas import tpu as pltpu
from jax.sharding import PartitionSpec as P

LEVELS = 6
SIDE = 4
TILE = 128
HALF = TILE // 2
CH = 3
ROWS = CH * TILE
PAIRED = CH * HALF
BOTH = ("row", "col")
AXES = dict(rows=8, cols=16)
BATCH = 4
LIMIT = 16 * 2**20
ROUTE_LIMIT = 56 * 2**20

STARTS = {1: 0, 2: 64, 3: 96, 4: 112, 5: 120, 6: 124}


def pooling_matrices():
    x = np.arange(TILE)
    pool = np.zeros((TILE, 3 * TILE), np.float32)
    spread = np.zeros((TILE, TILE), np.float32)
    for k in range(1, LEVELS):
        for i in range(TILE >> k):
            lane = STARTS[k] + i
            pool[(x >> k) == i, lane] = 0.25**k
            spread[lane, (x >> k) == i] = 1.0
            if k < LEVELS - 1:
                pool[(x >> (k + 1)) == (i >> 1), TILE + lane] = 0.25 ** (k + 1)
    for i in range(TILE):
        pool[(x >> 1) == (i >> 1), 2 * TILE + i] = 0.25
    twice = lambda m: np.concatenate([m, m], axis=0).astype(ml_dtypes.bfloat16)
    return twice(pool), twice(spread)


def split_two(value):
    high = value.astype(jnp.bfloat16)
    low = (value - high.astype(jnp.float32)).astype(jnp.bfloat16)
    return jnp.concatenate([high, low], axis=1)


def even(ref, count):
    return ref[pl.ds(0, count, stride=2), :]


def odd(ref, count):
    return ref[pl.ds(1, count, stride=2), :]


def slot_contribution(x_ref, label_ref, slot_ids, pool_ref, spread_ref, scratch):
    n = len(slot_ids)
    a_refs, b_refs, m_refs, w_refs, up_ref = scratch
    label_even, label_odd = even(label_ref, n * HALF), odd(label_ref, n * HALF)
    hit_even, hit_odd = [], []
    for j, slot in enumerate(slot_ids):
        hit_even.append(label_even[j * HALF : (j + 1) * HALF] == slot)
        hit_odd.append(label_odd[j * HALF : (j + 1) * HALF] == slot)
    one, zero = jnp.float32(1), jnp.float32(0)
    mask = jnp.concatenate(
        [jnp.where(e, one, zero) + jnp.where(o, one, zero) for e, o in zip(hit_even, hit_odd)], axis=0
    )
    rows_summed = even(x_ref, n * PAIRED) + odd(x_ref, n * PAIRED)
    pooled = jnp.dot(split_two(rows_summed), pool_ref[...], preferred_element_type=jnp.float32)
    a = {1: pooled[:, :TILE]}
    b = {1: pooled[:, TILE : 2 * TILE]}
    first = pooled[:, 2 * TILE :]
    m = {
        1: jnp.dot(
            mask.astype(jnp.bfloat16), pool_ref[:TILE, :TILE], preferred_element_type=jnp.float32
        )
    }
    for k in range(1, LEVELS - 1):
        for values, refs, rows in ((a, a_refs, n * PAIRED), (b, b_refs, n * PAIRED), (m, m_refs, n * HALF)):
            count = rows >> (k - 1)
            refs[k][...] = values[k]
            values[k + 1] = even(refs[k], count // 2) + odd(refs[k], count // 2)
    weights = {}
    for k in range(1, LEVELS):
        count = HALF >> (k - 1)
        for j in range(n):
            for c in range(CH):
                w_refs[k][pl.ds((j * CH + c) * count, count), :] = m[k][j * count : (j + 1) * count]
        weights[k] = w_refs[k][...]
    picture = None
    for k in range(LEVELS - 1, 0, -1):
        rows = (n * PAIRED) >> (k - 1)
        lane = lax.broadcasted_iota(jnp.int32, (rows, TILE), 1)
        inside = (lane >= STARTS[k]) & (lane < STARTS[k + 1])
        if k == LEVELS - 1:
            spread_up = jnp.zeros((rows, TILE), jnp.float32)
        else:
            lower = (lane[: rows // 2] >= STARTS[k]) & (lane[: rows // 2] < STARTS[k + 1])
            merged = jnp.where(lower, b[k + 1], picture)
            up_ref[pl.ds(0, rows // 2, stride=2), :] = merged
            up_ref[pl.ds(1, rows // 2, stride=2), :] = merged
            spread_up = up_ref[pl.ds(0, rows), :]
        weight = weights[k]
        banded = jnp.where(weight > 0, (a[k] - spread_up) * weight, zero)
        picture = jnp.where(inside, banded, spread_up)
    wide = jnp.dot(split_two(picture), spread_ref[...], preferred_element_type=jnp.float32)
    parts = ([], [])
    for j, slot in enumerate(slot_ids):
        for c in range(CH):
            rows = slice((j * CH + c) * HALF, (j * CH + c + 1) * HALF)
            for parity, part in enumerate(parts):
                hit = label_ref[pl.ds(j * TILE + parity, HALF, stride=2), :] == slot
                x = x_ref[pl.ds((j * CH + c) * TILE + parity, HALF, stride=2), :]
                part.append(jnp.where(hit, x - first[rows], zero) + wide[rows])
    return parts


def place(below):
    column = lax.axis_index("col")
    y, x = column // SIDE, column % SIDE
    along_x = lax.axis_index("row") % 2 == below
    return jnp.where(along_x, x, y), jnp.where(along_x, y, x), along_x


def blend_kernel(offsets, totals, groups, below, *refs):
    count = len(offsets)
    message_refs = refs[:count]
    label_ref, pool_ref, spread_ref = refs[count : count + 3]
    refs = refs[count + 3 :]
    sum_refs, refs = refs[:totals], refs[totals:]
    out_refs, refs = refs[:groups], refs[groups:]
    levels = LEVELS - 1
    a_refs = dict(zip(range(1, levels), refs[: levels - 1]))
    b_refs = dict(zip(range(1, levels), refs[levels - 1 : 2 * levels - 2]))
    m_refs = dict(zip(range(1, levels), refs[2 * levels - 2 : 3 * levels - 3]))
    w_refs = dict(zip(range(1, levels + 1), refs[3 * levels - 3 : 4 * levels - 3]))
    up_ref = refs[4 * levels - 3]
    scratch = (a_refs, b_refs, m_refs, w_refs, up_ref)
    near, far, along_x = place(below)
    slots = []
    for offset in offsets:
        from_near = (near - offset + SIDE) % SIDE
        source = jnp.where(along_x, far * SIDE + from_near, from_near * SIDE + far)
        slots.append(source + below * SIDE * SIDE)

    def step(i):
        even_sum = odd_sum = None
        labels = label_ref.at[pl.ds(i * BATCH * TILE, BATCH * TILE)]
        for message_ref, slot in zip(message_refs, slots):
            message = message_ref.at[pl.ds(i * BATCH * ROWS, BATCH * ROWS)]
            even_part, odd_part = slot_contribution(message, labels, [slot] * BATCH, pool_ref, spread_ref, scratch)
            even_sum = even_part if even_sum is None else [p + q for p, q in zip(even_sum, even_part)]
            odd_sum = odd_part if odd_sum is None else [p + q for p, q in zip(odd_sum, odd_part)]
        for j in range(BATCH):
            for c in range(CH):
                rows = pl.ds(c * HALF, HALF)
                for parity, part in ((0, even_sum), (1, odd_sum)):
                    value = part[j * CH + c]
                    for sum_ref in sum_refs:
                        value = value + sum_ref[i * BATCH + j, parity, rows, :]
                    if groups == 1:
                        out_refs[0][i * BATCH + j, parity, rows, :] = value
                    else:
                        out_refs[i * BATCH + j][parity, rows, :] = value

    if groups == 1:
        pl.loop(0, SIDE // BATCH)(step)
    else:
        for i in range(SIDE // BATCH):
            step(i)


def blend(messages, offsets, labels, matrices, totals, groups, below):
    part = (2, PAIRED, TILE)
    operands = list(messages) + [labels] + list(matrices) + list(totals)
    if groups == 1:
        out_shape = [jax.ShapeDtypeStruct((SIDE, *part), jnp.float32)]
    else:
        out_shape = [jax.ShapeDtypeStruct(part, jnp.float32) for _ in range(groups)]
    image = lambda rows: pltpu.VMEM((rows, TILE), jnp.float32)
    scratch = [image((BATCH * PAIRED) >> (k - 1)) for _ in range(2) for k in range(1, LEVELS - 1)]
    scratch += [image((BATCH * HALF) >> (k - 1)) for k in range(1, LEVELS - 1)]
    scratch += [image((BATCH * PAIRED) >> (k - 1)) for k in range(1, LEVELS)]
    scratch += [image(BATCH * PAIRED)]
    slots = SIDE * len(messages)
    whole = pl.BlockSpec(memory_space=pltpu.VMEM)
    out = pl.pallas_call(
        functools.partial(blend_kernel, offsets, len(totals), groups, below),
        in_specs=[whole] * len(operands),
        out_specs=[whole] * groups,
        scratch_shapes=scratch,
        out_shape=out_shape,
        compiler_params=pltpu.CompilerParams(vmem_limit_bytes=LIMIT),
        cost_estimate=pl.CostEstimate(
            flops=slots * PAIRED * 2 * 256 * 512, bytes_accessed=slots * ROWS * TILE * 12, transcendentals=0
        ),
    )(*operands)
    return out[0] if groups == 1 else out


def route_kernel(pieces, after, route_ref, block_ref, *refs):
    refs = refs[after:]
    out_refs, (found_ref, sem) = refs[: len(pieces)], refs[len(pieces) :]
    columns = SIDE * SIDE
    for q in range(2 * columns):
        found_ref[q] = -1
    for i in range(block_ref.shape[0]):
        found_ref[route_ref[0, i]] = i
    count = 0
    for out_ref, (d, below) in zip(out_refs, pieces):
        near, far, along_x = place(below)
        there = (near + d) % SIDE
        for slot in range(SIDE):
            across = (far + slot) % SIDE
            column = jnp.where(along_x, across * SIDE + there, there * SIDE + across)
            block = found_ref[below * columns + column]
            count += jnp.where(block >= 0, 1, 0)

            @pl.when(block >= 0)
            def _():
                pltpu.make_async_copy(block_ref.at[block], out_ref.at[slot], sem).start()

    @pl.loop(0, count)
    def _(_):
        pltpu.make_async_copy(block_ref.at[0], out_refs[0].at[0], sem).wait()


def route(blocks, routes, pieces, after=()):
    out_shape = [jax.ShapeDtypeStruct((SIDE, ROWS, TILE), jnp.float32) for _ in pieces]
    whole = pl.BlockSpec(memory_space=pltpu.VMEM)
    return pl.pallas_call(
        functools.partial(route_kernel, pieces, len(after)),
        in_specs=[pl.BlockSpec(memory_space=pltpu.SMEM), pl.BlockSpec(memory_space=pltpu.HBM)]
        + [whole] * len(after),
        out_specs=[whole] * len(out_shape),
        out_shape=out_shape,
        scratch_shapes=[pltpu.SMEM((2 * SIDE * SIDE,), jnp.int32), pltpu.SemaphoreType.DMA],
        compiler_params=pltpu.CompilerParams(vmem_limit_bytes=ROUTE_LIMIT),
        cost_estimate=pl.CostEstimate(flops=0, bytes_accessed=blocks.size * 4, transcendentals=0),
    )(routes, blocks, *after)


def finish_kernel(own_ref, first_ref, second_ref, third_ref, out_ref):
    for parity in range(2):
        total = own_ref[parity] + first_ref[parity] + second_ref[parity] + third_ref[parity]
        out_ref[pl.ds(parity, PAIRED, stride=2), :] = total


def finish(*parts):
    whole = pl.BlockSpec(memory_space=pltpu.VMEM)
    return pl.pallas_call(
        finish_kernel,
        in_specs=[whole] * len(parts),
        out_specs=whole,
        out_shape=jax.ShapeDtypeStruct((ROWS, TILE), jnp.float32),
        compiler_params=pltpu.CompilerParams(vmem_limit_bytes=LIMIT),
    )(*parts)


def pairs(phase, steps):
    result = []
    for r in range(AXES["rows"]):
        for c in range(AXES["cols"]):
            y, x = divmod(c, SIDE)
            if r % 2 == phase:
                x = (x + steps) % SIDE
            else:
                y = (y + steps) % SIDE
            result.append((r * AXES["cols"] + c, r * AXES["cols"] + y * SIDE + x))
    return result


def moved(value, phase, steps):
    return lax.ppermute(value, BOTH, pairs(phase, steps))


def shards(frame_blocks, block_routes, seam_labels):
    rows = AXES["rows"]
    matrices = [jnp.asarray(m) for m in pooling_matrices()]
    blocks = frame_blocks[0].reshape(-1, ROWS, TILE)
    labels = jnp.concatenate([seam_labels] + [moved(seam_labels, 1, -d) for d in range(1, SIDE)])
    labels_below = lax.ppermute(labels, "row", [(r + 1, r) for r in range(rows - 1)])
    near, routed = {}, []
    for pieces in ([(0, 1), (2, 1)], [(1, 1), (3, 1)], [(0, 0), (1, 0), (3, 0), (2, 0)]):
        after = [labels, *routed[:1]] if near else []
        routed = route(blocks, block_routes, pieces, after)
        for (d, below), value in zip(pieces, routed):
            near[d, below] = (moved(value, below, d) if d else value).reshape(-1, TILE)
    down, own = ([near[d, below] for d in (0, 2, 1, 3)] for below in (1, 0))
    total = blend(down[:2], (0, 2), labels_below, matrices, [], 1, 1)
    total = blend(down[2:], (1, 3), labels_below, matrices, [total], 1, 1)
    above = lax.ppermute(total, "row", [(r, r + 1) for r in range(rows - 1)])
    total = blend(own[:2], (0, 2), labels, matrices, [], 1, 0)
    parts = blend(own[2:], (1, 3), labels, matrices, [total, above], SIDE, 0)
    return finish(parts[0], *[moved(parts[d], 1, d) for d in (2, 1, 3)]).reshape(CH, TILE, TILE)


def solution(mesh):
    return jax.shard_map(
        shards,
        mesh=mesh,
        in_specs=(P("row", "col", None, None, None), P("row", "col"), P("row", "col")),
        out_specs=P(None, "row", "col"),
        check_vma=False,
    )
```

```python
import functools

import jax
import jax.numpy as jnp
import ml_dtypes
import numpy as np
from jax import lax
from jax.experimental import pallas as pl
from jax.experimental.pallas import tpu as pltpu
from jax.sharding import PartitionSpec as P

LEVELS = 6
SIDE = 4
TILE = 128
HALF = TILE // 2
CH = 3
ROWS = CH * TILE
PAIRED = CH * HALF
BOTH = ("row", "col")
AXES = dict(rows=8, cols=16)
BATCH = 4
LIMIT = 16 * 2**20
ROUTE_LIMIT = 56 * 2**20

STARTS = {1: 0, 2: 64, 3: 96, 4: 112, 5: 120, 6: 124}


def pooling_matrices():
    x = np.arange(TILE)
    pool = np.zeros((TILE, 3 * TILE), np.float32)
    spread = np.zeros((TILE, TILE), np.float32)
    for k in range(1, LEVELS):
        for i in range(TILE >> k):
            lane = STARTS[k] + i
            pool[(x >> k) == i, lane] = 0.25**k
            spread[lane, (x >> k) == i] = 1.0
            if k < LEVELS - 1:
                pool[(x >> (k + 1)) == (i >> 1), TILE + lane] = 0.25 ** (k + 1)
    for i in range(TILE):
        pool[(x >> 1) == (i >> 1), 2 * TILE + i] = 0.25
    twice = lambda m: np.concatenate([m, m], axis=0).astype(ml_dtypes.bfloat16)
    return twice(pool), twice(spread)


def split_two(value):
    high = value.astype(jnp.bfloat16)
    low = (value - high.astype(jnp.float32)).astype(jnp.bfloat16)
    return jnp.concatenate([high, low], axis=1)


def even(ref, count):
    return ref[pl.ds(0, count, stride=2), :]


def odd(ref, count):
    return ref[pl.ds(1, count, stride=2), :]


def slot_contribution(x_ref, label_ref, slot_ids, pool_ref, spread_ref, scratch):
    n = len(slot_ids)
    a_refs, b_refs, m_refs, w_refs, up_ref = scratch
    label_even, label_odd = even(label_ref, n * HALF), odd(label_ref, n * HALF)
    hit_even, hit_odd = [], []
    for j, slot in enumerate(slot_ids):
        hit_even.append(label_even[j * HALF : (j + 1) * HALF] == slot)
        hit_odd.append(label_odd[j * HALF : (j + 1) * HALF] == slot)
    one, zero = jnp.float32(1), jnp.float32(0)
    mask = jnp.concatenate(
        [jnp.where(e, one, zero) + jnp.where(o, one, zero) for e, o in zip(hit_even, hit_odd)], axis=0
    )
    rows_summed = even(x_ref, n * PAIRED) + odd(x_ref, n * PAIRED)
    pooled = jnp.dot(split_two(rows_summed), pool_ref[...], preferred_element_type=jnp.float32)
    a = {1: pooled[:, :TILE]}
    b = {1: pooled[:, TILE : 2 * TILE]}
    first = pooled[:, 2 * TILE :]
    m = {
        1: jnp.dot(
            mask.astype(jnp.bfloat16), pool_ref[:TILE, :TILE], preferred_element_type=jnp.float32
        )
    }
    for k in range(1, LEVELS - 1):
        for values, refs, rows in ((a, a_refs, n * PAIRED), (b, b_refs, n * PAIRED), (m, m_refs, n * HALF)):
            count = rows >> (k - 1)
            refs[k][...] = values[k]
            values[k + 1] = even(refs[k], count // 2) + odd(refs[k], count // 2)
    weights = {}
    for k in range(1, LEVELS):
        count = HALF >> (k - 1)
        for j in range(n):
            for c in range(CH):
                w_refs[k][pl.ds((j * CH + c) * count, count), :] = m[k][j * count : (j + 1) * count]
        weights[k] = w_refs[k][...]
    picture = None
    for k in range(LEVELS - 1, 0, -1):
        rows = (n * PAIRED) >> (k - 1)
        lane = lax.broadcasted_iota(jnp.int32, (rows, TILE), 1)
        inside = (lane >= STARTS[k]) & (lane < STARTS[k + 1])
        if k == LEVELS - 1:
            spread_up = jnp.zeros((rows, TILE), jnp.float32)
        else:
            lower = (lane[: rows // 2] >= STARTS[k]) & (lane[: rows // 2] < STARTS[k + 1])
            merged = jnp.where(lower, b[k + 1], picture)
            up_ref[pl.ds(0, rows // 2, stride=2), :] = merged
            up_ref[pl.ds(1, rows // 2, stride=2), :] = merged
            spread_up = up_ref[pl.ds(0, rows), :]
        weight = weights[k]
        banded = jnp.where(weight > 0, (a[k] - spread_up) * weight, zero)
        picture = jnp.where(inside, banded, spread_up)
    wide = jnp.dot(split_two(picture), spread_ref[...], preferred_element_type=jnp.float32)
    parts = ([], [])
    for j, slot in enumerate(slot_ids):
        for c in range(CH):
            rows = slice((j * CH + c) * HALF, (j * CH + c + 1) * HALF)
            for parity, part in enumerate(parts):
                hit = label_ref[pl.ds(j * TILE + parity, HALF, stride=2), :] == slot
                x = x_ref[pl.ds((j * CH + c) * TILE + parity, HALF, stride=2), :]
                part.append(jnp.where(hit, x - first[rows], zero) + wide[rows])
    return parts


def place(below):
    column = lax.axis_index("col")
    y, x = column // SIDE, column % SIDE
    along_x = lax.axis_index("row") % 2 == below
    return jnp.where(along_x, x, y), jnp.where(along_x, y, x), along_x


def blend_kernel(offsets, totals, groups, below, *refs):
    count = len(offsets)
    message_refs = refs[:count]
    label_ref, pool_ref, spread_ref = refs[count : count + 3]
    refs = refs[count + 3 :]
    sum_refs, refs = refs[:totals], refs[totals:]
    out_refs, refs = refs[:groups], refs[groups:]
    levels = LEVELS - 1
    a_refs = dict(zip(range(1, levels), refs[: levels - 1]))
    b_refs = dict(zip(range(1, levels), refs[levels - 1 : 2 * levels - 2]))
    m_refs = dict(zip(range(1, levels), refs[2 * levels - 2 : 3 * levels - 3]))
    w_refs = dict(zip(range(1, levels + 1), refs[3 * levels - 3 : 4 * levels - 3]))
    up_ref = refs[4 * levels - 3]
    scratch = (a_refs, b_refs, m_refs, w_refs, up_ref)
    near, far, along_x = place(below)
    slots = []
    for offset in offsets:
        from_near = (near - offset + SIDE) % SIDE
        source = jnp.where(along_x, far * SIDE + from_near, from_near * SIDE + far)
        slots.append(source + below * SIDE * SIDE)

    def step(i):
        even_sum = odd_sum = None
        labels = label_ref.at[pl.ds(i * BATCH * TILE, BATCH * TILE)]
        for message_ref, slot in zip(message_refs, slots):
            message = message_ref.at[pl.ds(i * BATCH * ROWS, BATCH * ROWS)]
            even_part, odd_part = slot_contribution(message, labels, [slot] * BATCH, pool_ref, spread_ref, scratch)
            even_sum = even_part if even_sum is None else [p + q for p, q in zip(even_sum, even_part)]
            odd_sum = odd_part if odd_sum is None else [p + q for p, q in zip(odd_sum, odd_part)]
        for j in range(BATCH):
            for c in range(CH):
                rows = pl.ds(c * HALF, HALF)
                for parity, part in ((0, even_sum), (1, odd_sum)):
                    value = part[j * CH + c]
                    for sum_ref in sum_refs:
                        value = value + sum_ref[i * BATCH + j, parity, rows, :]
                    if groups == 1:
                        out_refs[0][i * BATCH + j, parity, rows, :] = value
                    else:
                        out_refs[i * BATCH + j][parity, rows, :] = value

    if groups == 1:
        pl.loop(0, SIDE // BATCH)(step)
    else:
        for i in range(SIDE // BATCH):
            step(i)


def blend(messages, offsets, labels, matrices, totals, groups, below):
    part = (2, PAIRED, TILE)
    operands = list(messages) + [labels] + list(matrices) + list(totals)
    if groups == 1:
        out_shape = [jax.ShapeDtypeStruct((SIDE, *part), jnp.float32)]
    else:
        out_shape = [jax.ShapeDtypeStruct(part, jnp.float32) for _ in range(groups)]
    image = lambda rows: pltpu.VMEM((rows, TILE), jnp.float32)
    scratch = [image((BATCH * PAIRED) >> (k - 1)) for _ in range(2) for k in range(1, LEVELS - 1)]
    scratch += [image((BATCH * HALF) >> (k - 1)) for k in range(1, LEVELS - 1)]
    scratch += [image((BATCH * PAIRED) >> (k - 1)) for k in range(1, LEVELS)]
    scratch += [image(BATCH * PAIRED)]
    slots = SIDE * len(messages)
    whole = pl.BlockSpec(memory_space=pltpu.VMEM)
    out = pl.pallas_call(
        functools.partial(blend_kernel, offsets, len(totals), groups, below),
        in_specs=[whole] * len(operands),
        out_specs=[whole] * groups,
        scratch_shapes=scratch,
        out_shape=out_shape,
        compiler_params=pltpu.CompilerParams(vmem_limit_bytes=LIMIT),
        cost_estimate=pl.CostEstimate(
            flops=slots * PAIRED * 2 * 256 * 512, bytes_accessed=slots * ROWS * TILE * 12, transcendentals=0
        ),
    )(*operands)
    return out[0] if groups == 1 else out


def route_kernel(pieces, after, route_ref, block_ref, *refs):
    refs = refs[after:]
    out_refs, (found_ref, sem) = refs[: len(pieces)], refs[len(pieces) :]
    columns = SIDE * SIDE
    for q in range(2 * columns):
        found_ref[q] = -1
    for i in range(block_ref.shape[0]):
        found_ref[route_ref[0, i]] = i
    count = 0
    for out_ref, (d, below) in zip(out_refs, pieces):
        near, far, along_x = place(below)
        there = (near + d) % SIDE
        for slot in range(SIDE):
            across = (far + slot) % SIDE
            column = jnp.where(along_x, across * SIDE + there, there * SIDE + across)
            block = found_ref[below * columns + column]
            count += jnp.where(block >= 0, 1, 0)

            @pl.when(block >= 0)
            def _():
                pltpu.make_async_copy(block_ref.at[block], out_ref.at[slot], sem).start()

    @pl.loop(0, count)
    def _(_):
        pltpu.make_async_copy(block_ref.at[0], out_refs[0].at[0], sem).wait()


def route(blocks, routes, pieces, after=()):
    out_shape = [jax.ShapeDtypeStruct((SIDE, ROWS, TILE), jnp.float32) for _ in pieces]
    whole = pl.BlockSpec(memory_space=pltpu.VMEM)
    return pl.pallas_call(
        functools.partial(route_kernel, pieces, len(after)),
        in_specs=[pl.BlockSpec(memory_space=pltpu.SMEM), pl.BlockSpec(memory_space=pltpu.HBM)]
        + [whole] * len(after),
        out_specs=[whole] * len(out_shape),
        out_shape=out_shape,
        scratch_shapes=[pltpu.SMEM((2 * SIDE * SIDE,), jnp.int32), pltpu.SemaphoreType.DMA],
        compiler_params=pltpu.CompilerParams(vmem_limit_bytes=ROUTE_LIMIT),
        cost_estimate=pl.CostEstimate(flops=0, bytes_accessed=blocks.size * 4, transcendentals=0),
    )(routes, blocks, *after)


def finish_kernel(own_ref, first_ref, second_ref, third_ref, out_ref):
    for parity in range(2):
        total = own_ref[parity] + first_ref[parity] + second_ref[parity] + third_ref[parity]
        out_ref[pl.ds(parity, PAIRED, stride=2), :] = total


def finish(*parts):
    whole = pl.BlockSpec(memory_space=pltpu.VMEM)
    return pl.pallas_call(
        finish_kernel,
        in_specs=[whole] * len(parts),
        out_specs=whole,
        out_shape=jax.ShapeDtypeStruct((ROWS, TILE), jnp.float32),
        compiler_params=pltpu.CompilerParams(vmem_limit_bytes=LIMIT),
    )(*parts)


def pairs(phase, steps):
    result = []
    for r in range(AXES["rows"]):
        for c in range(AXES["cols"]):
            y, x = divmod(c, SIDE)
            if r % 2 == phase:
                x = (x + steps) % SIDE
            else:
                y = (y + steps) % SIDE
            result.append((r * AXES["cols"] + c, r * AXES["cols"] + y * SIDE + x))
    return result


def moved(value, phase, steps):
    return lax.ppermute(value, BOTH, pairs(phase, steps))


def shards(frame_blocks, block_routes, seam_labels):
    rows = AXES["rows"]
    matrices = [jnp.asarray(m) for m in pooling_matrices()]
    blocks = frame_blocks[0].reshape(-1, ROWS, TILE)
    labels = jnp.concatenate([seam_labels] + [moved(seam_labels, 1, -d) for d in range(1, SIDE)])
    labels_below = lax.ppermute(labels, "row", [(r + 1, r) for r in range(rows - 1)])
    near, routed = {}, []
    for pieces in ([(0, 1), (2, 1)], [(1, 1), (3, 1)], [(0, 0), (1, 0), (3, 0), (2, 0)]):
        after = [labels, *routed[:1]] if near else []
        routed = route(blocks, block_routes, pieces, after)
        for (d, below), value in zip(pieces, routed):
            near[d, below] = (moved(value, below, d) if d else value).reshape(-1, TILE)
    down, own = ([near[d, below] for d in (0, 2, 1, 3)] for below in (1, 0))
    total = blend(down[:2], (0, 2), labels_below, matrices, [], 1, 1)
    total = blend(down[2:], (1, 3), labels_below, matrices, [total], 1, 1)
    above = lax.ppermute(total, "row", [(r, r + 1) for r in range(rows - 1)])
    total = blend(own[:1], (0,), labels, matrices, [], 1, 0)
    parts = blend([own[2], own[3], own[1]], (1, 3, 2), labels, matrices, [total, above], SIDE, 0)
    return finish(parts[0], *[moved(parts[d], 1, d) for d in (2, 1, 3)]).reshape(CH, TILE, TILE)


def solution(mesh):
    return jax.shard_map(
        shards,
        mesh=mesh,
        in_specs=(P("row", "col", None, None, None), P("row", "col"), P("row", "col")),
        out_specs=P(None, "row", "col"),
        check_vma=False,
    )
```

```python
import functools

import jax
import jax.numpy as jnp
import ml_dtypes
import numpy as np
from jax import lax
from jax.experimental import pallas as pl
from jax.experimental.pallas import tpu as pltpu
from jax.sharding import PartitionSpec as P

LEVELS = 6
SIDE = 4
TILE = 128
HALF = TILE // 2
CH = 3
ROWS = CH * TILE
PAIRED = CH * HALF
BOTH = ("row", "col")
AXES = dict(rows=8, cols=16)
BATCH = 4
LIMIT = 16 * 2**20
ROUTE_LIMIT = 56 * 2**20

STARTS = {1: 0, 2: 64, 3: 96, 4: 112, 5: 120, 6: 124}


def pooling_matrices():
    x = np.arange(TILE)
    pool = np.zeros((TILE, 3 * TILE), np.float32)
    spread = np.zeros((TILE, TILE), np.float32)
    for k in range(1, LEVELS):
        for i in range(TILE >> k):
            lane = STARTS[k] + i
            pool[(x >> k) == i, lane] = 0.25**k
            spread[lane, (x >> k) == i] = 1.0
            if k < LEVELS - 1:
                pool[(x >> (k + 1)) == (i >> 1), TILE + lane] = 0.25 ** (k + 1)
    for i in range(TILE):
        pool[(x >> 1) == (i >> 1), 2 * TILE + i] = 0.25
    twice = lambda m: np.concatenate([m, m], axis=0).astype(ml_dtypes.bfloat16)
    return twice(pool), twice(spread)


def split_two(value):
    high = value.astype(jnp.bfloat16)
    low = (value - high.astype(jnp.float32)).astype(jnp.bfloat16)
    return jnp.concatenate([high, low], axis=1)


def even(ref, count):
    return ref[pl.ds(0, count, stride=2), :]


def odd(ref, count):
    return ref[pl.ds(1, count, stride=2), :]


def slot_contribution(x_ref, label_ref, slot_ids, pool_ref, spread_ref, scratch):
    n = len(slot_ids)
    a_refs, b_refs, m_refs, w_refs, up_ref = scratch
    label_even, label_odd = even(label_ref, n * HALF), odd(label_ref, n * HALF)
    hit_even, hit_odd = [], []
    for j, slot in enumerate(slot_ids):
        hit_even.append(label_even[j * HALF : (j + 1) * HALF] == slot)
        hit_odd.append(label_odd[j * HALF : (j + 1) * HALF] == slot)
    one, zero = jnp.float32(1), jnp.float32(0)
    mask = jnp.concatenate(
        [jnp.where(e, one, zero) + jnp.where(o, one, zero) for e, o in zip(hit_even, hit_odd)], axis=0
    )
    rows_summed = even(x_ref, n * PAIRED) + odd(x_ref, n * PAIRED)
    pooled = jnp.dot(split_two(rows_summed), pool_ref[...], preferred_element_type=jnp.float32)
    a = {1: pooled[:, :TILE]}
    b = {1: pooled[:, TILE : 2 * TILE]}
    first = pooled[:, 2 * TILE :]
    m = {
        1: jnp.dot(
            mask.astype(jnp.bfloat16), pool_ref[:TILE, :TILE], preferred_element_type=jnp.float32
        )
    }
    for k in range(1, LEVELS - 1):
        for values, refs, rows in ((a, a_refs, n * PAIRED), (b, b_refs, n * PAIRED), (m, m_refs, n * HALF)):
            count = rows >> (k - 1)
            refs[k][...] = values[k]
            values[k + 1] = even(refs[k], count // 2) + odd(refs[k], count // 2)
    weights = {}
    for k in range(1, LEVELS):
        count = HALF >> (k - 1)
        for j in range(n):
            for c in range(CH):
                w_refs[k][pl.ds((j * CH + c) * count, count), :] = m[k][j * count : (j + 1) * count]
        weights[k] = w_refs[k][...]
    picture = None
    for k in range(LEVELS - 1, 0, -1):
        rows = (n * PAIRED) >> (k - 1)
        lane = lax.broadcasted_iota(jnp.int32, (rows, TILE), 1)
        inside = (lane >= STARTS[k]) & (lane < STARTS[k + 1])
        if k == LEVELS - 1:
            spread_up = jnp.zeros((rows, TILE), jnp.float32)
        else:
            lower = (lane[: rows // 2] >= STARTS[k]) & (lane[: rows // 2] < STARTS[k + 1])
            merged = jnp.where(lower, b[k + 1], picture)
            up_ref[pl.ds(0, rows // 2, stride=2), :] = merged
            up_ref[pl.ds(1, rows // 2, stride=2), :] = merged
            spread_up = up_ref[pl.ds(0, rows), :]
        weight = weights[k]
        banded = jnp.where(weight > 0, (a[k] - spread_up) * weight, zero)
        picture = jnp.where(inside, banded, spread_up)
    wide = jnp.dot(split_two(picture), spread_ref[...], preferred_element_type=jnp.float32)
    parts = ([], [])
    for j, slot in enumerate(slot_ids):
        for c in range(CH):
            rows = slice((j * CH + c) * HALF, (j * CH + c + 1) * HALF)
            for parity, part in enumerate(parts):
                hit = label_ref[pl.ds(j * TILE + parity, HALF, stride=2), :] == slot
                x = x_ref[pl.ds((j * CH + c) * TILE + parity, HALF, stride=2), :]
                part.append(jnp.where(hit, x - first[rows], zero) + wide[rows])
    return parts


def place(below):
    column = lax.axis_index("col")
    y, x = column // SIDE, column % SIDE
    along_x = lax.axis_index("row") % 2 == below
    return jnp.where(along_x, x, y), jnp.where(along_x, y, x), along_x


def blend_kernel(offsets, totals, groups, below, *refs):
    count = len(offsets)
    message_refs = refs[:count]
    label_ref, pool_ref, spread_ref = refs[count : count + 3]
    refs = refs[count + 3 :]
    sum_refs, refs = refs[:totals], refs[totals:]
    out_refs, refs = refs[:groups], refs[groups:]
    levels = LEVELS - 1
    a_refs = dict(zip(range(1, levels), refs[: levels - 1]))
    b_refs = dict(zip(range(1, levels), refs[levels - 1 : 2 * levels - 2]))
    m_refs = dict(zip(range(1, levels), refs[2 * levels - 2 : 3 * levels - 3]))
    w_refs = dict(zip(range(1, levels + 1), refs[3 * levels - 3 : 4 * levels - 3]))
    up_ref = refs[4 * levels - 3]
    scratch = (a_refs, b_refs, m_refs, w_refs, up_ref)
    near, far, along_x = place(below)
    slots = []
    for offset in offsets:
        from_near = (near - offset + SIDE) % SIDE
        source = jnp.where(along_x, far * SIDE + from_near, from_near * SIDE + far)
        slots.append(source + below * SIDE * SIDE)

    def step(i):
        even_sum = odd_sum = None
        labels = label_ref.at[pl.ds(i * BATCH * TILE, BATCH * TILE)]
        for message_ref, slot in zip(message_refs, slots):
            message = message_ref.at[pl.ds(i * BATCH * ROWS, BATCH * ROWS)]
            even_part, odd_part = slot_contribution(message, labels, [slot] * BATCH, pool_ref, spread_ref, scratch)
            even_sum = even_part if even_sum is None else [p + q for p, q in zip(even_sum, even_part)]
            odd_sum = odd_part if odd_sum is None else [p + q for p, q in zip(odd_sum, odd_part)]
        for j in range(BATCH):
            for c in range(CH):
                rows = pl.ds(c * HALF, HALF)
                for parity, part in ((0, even_sum), (1, odd_sum)):
                    value = part[j * CH + c]
                    for sum_ref in sum_refs:
                        value = value + sum_ref[i * BATCH + j, parity, rows, :]
                    if groups == 1:
                        out_refs[0][i * BATCH + j, parity, rows, :] = value
                    else:
                        out_refs[i * BATCH + j][parity, rows, :] = value

    if groups == 1:
        pl.loop(0, SIDE // BATCH)(step)
    else:
        for i in range(SIDE // BATCH):
            step(i)


def blend(messages, offsets, labels, matrices, totals, groups, below):
    part = (2, PAIRED, TILE)
    operands = list(messages) + [labels] + list(matrices) + list(totals)
    if groups == 1:
        out_shape = [jax.ShapeDtypeStruct((SIDE, *part), jnp.float32)]
    else:
        out_shape = [jax.ShapeDtypeStruct(part, jnp.float32) for _ in range(groups)]
    image = lambda rows: pltpu.VMEM((rows, TILE), jnp.float32)
    scratch = [image((BATCH * PAIRED) >> (k - 1)) for _ in range(2) for k in range(1, LEVELS - 1)]
    scratch += [image((BATCH * HALF) >> (k - 1)) for k in range(1, LEVELS - 1)]
    scratch += [image((BATCH * PAIRED) >> (k - 1)) for k in range(1, LEVELS)]
    scratch += [image(BATCH * PAIRED)]
    slots = SIDE * len(messages)
    whole = pl.BlockSpec(memory_space=pltpu.VMEM)
    out = pl.pallas_call(
        functools.partial(blend_kernel, offsets, len(totals), groups, below),
        in_specs=[whole] * len(operands),
        out_specs=[whole] * groups,
        scratch_shapes=scratch,
        out_shape=out_shape,
        compiler_params=pltpu.CompilerParams(vmem_limit_bytes=LIMIT),
        cost_estimate=pl.CostEstimate(
            flops=slots * PAIRED * 2 * 256 * 512, bytes_accessed=slots * ROWS * TILE * 12, transcendentals=0
        ),
    )(*operands)
    return out[0] if groups == 1 else out


def route_kernel(pieces, after, route_ref, block_ref, *refs):
    refs = refs[after:]
    out_refs, (found_ref, sem) = refs[: len(pieces)], refs[len(pieces) :]
    columns = SIDE * SIDE
    for q in range(2 * columns):
        found_ref[q] = -1
    for i in range(block_ref.shape[0]):
        found_ref[route_ref[0, i]] = i
    count = 0
    for out_ref, (d, below) in zip(out_refs, pieces):
        near, far, along_x = place(below)
        there = (near + d) % SIDE
        for slot in range(SIDE):
            across = (far + slot) % SIDE
            column = jnp.where(along_x, across * SIDE + there, there * SIDE + across)
            block = found_ref[below * columns + column]
            count += jnp.where(block >= 0, 1, 0)

            @pl.when(block >= 0)
            def _():
                pltpu.make_async_copy(block_ref.at[block], out_ref.at[slot], sem).start()

    @pl.loop(0, count)
    def _(_):
        pltpu.make_async_copy(block_ref.at[0], out_refs[0].at[0], sem).wait()


def route(blocks, routes, pieces, after=()):
    out_shape = [jax.ShapeDtypeStruct((SIDE, ROWS, TILE), jnp.float32) for _ in pieces]
    whole = pl.BlockSpec(memory_space=pltpu.VMEM)
    return pl.pallas_call(
        functools.partial(route_kernel, pieces, len(after)),
        in_specs=[pl.BlockSpec(memory_space=pltpu.SMEM), pl.BlockSpec(memory_space=pltpu.HBM)]
        + [pl.BlockSpec(memory_space=pl.ANY)] * len(after),
        out_specs=[whole] * len(out_shape),
        out_shape=out_shape,
        scratch_shapes=[pltpu.SMEM((2 * SIDE * SIDE,), jnp.int32), pltpu.SemaphoreType.DMA],
        compiler_params=pltpu.CompilerParams(vmem_limit_bytes=ROUTE_LIMIT),
        cost_estimate=pl.CostEstimate(flops=0, bytes_accessed=blocks.size * 4, transcendentals=0),
    )(routes, blocks, *after)


def finish_kernel(own_ref, first_ref, second_ref, third_ref, out_ref):
    for parity in range(2):
        total = own_ref[parity] + first_ref[parity] + second_ref[parity] + third_ref[parity]
        out_ref[pl.ds(parity, PAIRED, stride=2), :] = total


def finish(*parts):
    whole = pl.BlockSpec(memory_space=pltpu.VMEM)
    return pl.pallas_call(
        finish_kernel,
        in_specs=[whole] * len(parts),
        out_specs=whole,
        out_shape=jax.ShapeDtypeStruct((ROWS, TILE), jnp.float32),
        compiler_params=pltpu.CompilerParams(vmem_limit_bytes=LIMIT),
    )(*parts)


def pairs(phase, steps):
    result = []
    for r in range(AXES["rows"]):
        for c in range(AXES["cols"]):
            y, x = divmod(c, SIDE)
            if r % 2 == phase:
                x = (x + steps) % SIDE
            else:
                y = (y + steps) % SIDE
            result.append((r * AXES["cols"] + c, r * AXES["cols"] + y * SIDE + x))
    return result


def moved(value, phase, steps):
    return lax.ppermute(value, BOTH, pairs(phase, steps))


def shards(frame_blocks, block_routes, seam_labels):
    rows = AXES["rows"]
    matrices = [jnp.asarray(m) for m in pooling_matrices()]
    blocks = frame_blocks[0].reshape(-1, ROWS, TILE)
    labels = jnp.concatenate([seam_labels] + [moved(seam_labels, 1, -d) for d in range(1, SIDE)])
    labels_below = lax.ppermute(labels, "row", [(r + 1, r) for r in range(rows - 1)])
    near, routed = {}, []
    for pieces in ([(0, 1), (2, 1)], [(1, 1), (3, 1)], [(0, 0), (1, 0), (3, 0), (2, 0)]):
        after = [labels, *routed[:1]] if near else []
        routed = route(blocks, block_routes, pieces, after)
        for (d, below), value in zip(pieces, routed):
            near[d, below] = (moved(value, below, d) if d else value).reshape(-1, TILE)
    down, own = ([near[d, below] for d in (0, 2, 1, 3)] for below in (1, 0))
    total = blend(down[:2], (0, 2), labels_below, matrices, [], 1, 1)
    total = blend(down[2:], (1, 3), labels_below, matrices, [total], 1, 1)
    above = lax.ppermute(total, "row", [(r, r + 1) for r in range(rows - 1)])
    total = blend(own[:1], (0,), labels, matrices, [], 1, 0)
    parts = blend([own[2], own[3], own[1]], (1, 3, 2), labels, matrices, [total, above], SIDE, 0)
    return finish(parts[0], *[moved(parts[d], 1, d) for d in (2, 1, 3)]).reshape(CH, TILE, TILE)


def solution(mesh):
    return jax.shard_map(
        shards,
        mesh=mesh,
        in_specs=(P("row", "col", None, None, None), P("row", "col"), P("row", "col")),
        out_specs=P(None, "row", "col"),
        check_vma=False,
    )
```
